128 devices in a mesh: dp: 16 (over y, z), seq: 8 (over x, core).
Axes of the slice: x: 4, y: 4, z: 4, core: 2. Of those that a mesh axis runs over, the one named last changes fastest.
Arguments:
- block_input: bfloat16 [16, 8, 256, 1408], P('dp', 'seq'), may hold values from -6 to 6
- norm_gain: float32 [1408], replicated, may hold values from 0.5 to 1.5
- qkv_weight: bfloat16 [1408, 4224], replicated, may hold values from -0.15625 to 0.15625
- frame_clip: int32 [16, 8], P('dp', 'seq'), may hold values from 0 to 2, never falling along the last dimension, each value on 1 to 4 neighbouring positions
- out_grad: bfloat16 [16, 8, 256, 1408], P('dp', 'seq'), may hold values from -6 to 6
Outputs:
- input_grad: bfloat16 [16, 8, 256, 1408], P('dp', 'seq')
- weight_grad: float32 [1408, 1408], P(('dp', 'seq'))
- gain_grad: float32 [1408], replicated
The draws below stay inside these ranges and needn't reach their ends.
Inputs may be any that keep to these rules, and one draw needn't show every extreme that they name: `frame_clip`: in each group the frames hold clips 0 to 2 in order, each of 1 to 4 frames, one exactly 4.
All inputs are finite; a program needn't handle non-finite values.
Results may differ from the reference program's by a relative error of at most 0.018.
Values may be sent and summed in bfloat16 or wider, within the bound.
No kernel may reach another device: no remote copies, remote signals or barrier semaphores. Data moves between devices by JAX's collectives and lax.ppermute only.
A program may use at most 128 MiB of HBM per device.

```python
import math
import jax
import jax.numpy as jnp
import numpy as np
from jax import lax

D = 1408
HEADS = 16
PATCHES = 256
GROUP_FRAMES = 8
GROUPS = 16
TOKENS = 32768
CLIPS = 3
MOST_FRAMES = 4


def steps_of(key, extent, shards, low, high):
    def one(position, blocks):
        steps = jax.random.uniform(jax.random.fold_in(jax.random.fold_in(key, 6), position), (blocks,), jnp.float32, low / len(shards), high / len(shards))
        return jnp.repeat(jnp.exp(steps), extent[position] // blocks).reshape((-1,) + (1,) * (len(extent) - position - 1))

    level = one(*shards[0])
    for cut in shards[1:]:
        level = level * one(*cut)
    return level


def length_profile(amount, total, bound, slope):
    portions = [(1 << 20) // math.isqrt(grade ** slope) + 1 for grade in range(2, amount + 1)]
    spare, counts = total - bound - (amount - 1), [1] * (amount - 1)
    while spare > 0:
        movable = [i for i in range(amount - 1) if counts[i] < bound]
        pool, remaining = sum([portions[i] for i in movable]), spare
        for i in movable:
            extra = min(bound - counts[i], max(1, remaining * portions[i] // pool), spare)
            counts[i] = counts[i] + extra
            spare = spare - extra
    return np.array([bound] + counts)


def uneven(own_key, number_of, total, limit, slope):
    if number_of == 2:
        one = jax.random.randint(own_key, (), max(1, total - limit), min(limit, total - 1) + 1)
        return jnp.stack([one, total - one])
    lengths = jnp.asarray(length_profile(number_of, total, limit, slope), jnp.int32)
    pairs = (number_of - 1) // 2
    donor, taker = lengths[1:1 + 2 * pairs:2], lengths[2:2 + 2 * pairs:2]
    room = jnp.minimum(donor - 1, limit - taker)
    shifted = jax.random.randint(jax.random.fold_in(own_key, 1), (pairs,), 0, 1 << 20) % (room + 1)
    lengths = lengths.at[1:1 + 2 * pairs:2].set(donor - shifted).at[2:2 + 2 * pairs:2].set(taker + shifted)
    return lengths[jax.random.permutation(jax.random.fold_in(own_key, 2), number_of)]


def scatter_about(own_key, dims, deviation, most, cuts=(), dtype=jnp.bfloat16):
    entries = deviation * jax.random.normal(own_key, dims, jnp.float32)
    if cuts:
        entries = entries * steps_of(own_key, dims, cuts, -0.22, 0.18)
    return jnp.clip(entries, -most, most).astype(dtype)


def setup_inputs(seed: int = 0) -> dict:
    arg_keys = jax.random.split(jax.random.key(seed), 6)
    return {
        "block_input": scatter_about(arg_keys[0], (GROUPS, GROUP_FRAMES, PATCHES, D), 1.0, 6.0, ((0, 16), (1, 8))),
        "norm_gain": jnp.clip(1.0 + 0.1 * jax.random.normal(arg_keys[1], (D,), jnp.float32), 0.5, 1.5),
        "qkv_weight": scatter_about(arg_keys[2], (D, 3 * D), D ** -0.5, 0.15625),
        "frame_clip": jax.vmap(lambda own: jnp.searchsorted(jnp.cumsum(uneven(own, CLIPS, GROUP_FRAMES, MOST_FRAMES, 1)), jnp.arange(GROUP_FRAMES), side="right"))(jax.random.split(arg_keys[3], GROUPS)).reshape((GROUPS, GROUP_FRAMES)).astype(jnp.int32),
        "out_grad": scatter_about(arg_keys[4], (GROUPS, GROUP_FRAMES, PATCHES, D), 1.0, 6.0, ((0, 16), (1, 8))),
    }


epsilon = 1e-06

def attention_grad(projected, incoming, same_clip):
    frames_all, positions, triple = projected.shape
    width = triple // 3
    head_dim = width // HEADS
    blocks = projected.astype(jnp.float32).reshape(frames_all, positions, 3, HEADS, head_dim)
    query_part = blocks[:, :, 0]
    key_part = blocks[:, :, 1]
    value_part = blocks[:, :, 2]
    outgrad = incoming.astype(jnp.float32).reshape(frames_all, positions, HEADS, head_dim)
    scaling = head_dim ** (-0.5)
    scores = jnp.einsum('fphd,gphd->phfg', query_part, key_part) * scaling
    largest = lax.optimization_barrier(jnp.max(jnp.where(same_clip, scores, -jnp.inf), axis=-1, keepdims=True))
    powers = jnp.where(same_clip, jnp.exp(scores - largest), 0.0)
    softmaxed = powers / lax.optimization_barrier(jnp.sum(powers, axis=-1, keepdims=True))
    rounded_probs = lax.optimization_barrier(softmaxed.astype(jnp.bfloat16)).astype(jnp.float32)
    d_value = jnp.einsum('phfg,fphd->gphd', rounded_probs, outgrad)
    d_probs = jnp.einsum('fphd,gphd->phfg', outgrad, value_part)
    row_dot = lax.optimization_barrier(jnp.sum(softmaxed * d_probs, axis=-1, keepdims=True))
    d_scores = (softmaxed * (d_probs - row_dot) * scaling).astype(jnp.bfloat16)
    d_scores = lax.optimization_barrier(d_scores).astype(jnp.float32)
    d_query = jnp.einsum('phfg,gphd->fphd', d_scores, key_part)
    d_key = jnp.einsum('phfg,fphd->gphd', d_scores, query_part)
    stacked = jnp.stack([d_query, d_key, d_value], axis=2)
    return stacked.reshape(frames_all, positions, triple).astype(jnp.bfloat16)

def reference(block_input, norm_gain, qkv_weight, frame_clip, out_grad):
    width = qkv_weight.shape[0]

    def group_backward(carry, inputs):
        weight_acc, gain_acc = carry
        frames_in, clip_ids, grads_in = inputs
        inputs_f = frames_in.astype(jnp.float32)
        centered = inputs_f - lax.optimization_barrier(jnp.mean(inputs_f, axis=-1, keepdims=True))
        inv_std = lax.rsqrt(lax.optimization_barrier(jnp.mean(centered * centered, axis=-1, keepdims=True)) + epsilon)
        normalized = centered * inv_std
        normed = (normalized * norm_gain).astype(jnp.bfloat16)
        normed_rows = normed.reshape(-1, width)
        projected = jnp.dot(normed_rows, qkv_weight, preferred_element_type=jnp.float32).astype(jnp.bfloat16)
        projected = projected.reshape(frames_in.shape[0], frames_in.shape[1], 3 * width)
        same_clip = clip_ids[:, None] == clip_ids[None, :]
        grads_qkv = attention_grad(projected, grads_in, same_clip)
        grad_rows = grads_qkv.reshape(-1, 3 * width)
        weight_acc = weight_acc + jnp.dot(normed_rows.T, grad_rows[:, 2 * width:], preferred_element_type=jnp.float32)
        d_normed = jnp.dot(grad_rows, qkv_weight.T, preferred_element_type=jnp.float32).reshape(frames_in.shape)
        gain_acc = gain_acc + lax.optimization_barrier(jnp.sum(d_normed * normalized, axis=(0, 1)))
        d_hat = d_normed * norm_gain
        first_mean = lax.optimization_barrier(jnp.mean(d_hat, axis=-1, keepdims=True))
        second_mean = lax.optimization_barrier(jnp.mean(d_hat * normalized, axis=-1, keepdims=True))
        input_grad = (inv_std * (d_hat - first_mean - normalized * second_mean)).astype(jnp.bfloat16)
        return ((weight_acc, gain_acc), input_grad)
    start_carry = (jnp.zeros((width, width), jnp.float32), jnp.zeros((width,), jnp.float32))
    (weight_sum, gain_sum), input_grad = lax.scan(group_backward, start_carry, (block_input, frame_clip, out_grad))
    factor = TOKENS ** (-0.5)
    return (input_grad, weight_sum * factor, gain_sum * factor)
```

```python
import jax
import jax.numpy as jnp
from jax import lax
from jax.experimental import pallas as pl
from jax.experimental.pallas import tpu as pltpu
from jax.sharding import PartitionSpec as P

HEADS = 16
HEAD_DIM = 88
D = 1408
TRIPLE = 3 * D
WIN = 256
PADDED = TRIPLE + 128
WIDE = D + 128
ROWS = 256
CHUNK = 32
SLOTS = 8
TILE = 256
BLOCK = 88
HALF = 768
EPSILON = 1e-06
SCALING = HEAD_DIM ** (-0.5)
MASKED = -1e30

BF = jnp.bfloat16
F32 = jnp.float32


def shape(dims, dtype):
    return jax.ShapeDtypeStruct(dims, dtype)


def call(body, outs, scratch=(), in_specs=None, mib=16, flops=0, data=0, name=None):
    extra = {} if in_specs is None else {"in_specs": in_specs}
    return pl.pallas_call(
        body,
        out_shape=outs,
        scratch_shapes=list(scratch),
        compiler_params=pltpu.CompilerParams(vmem_limit_bytes=mib << 20),
        cost_estimate=pl.CostEstimate(flops=flops, bytes_accessed=data, transcendentals=0),
        name=name,
        **extra,
    )


VMEM = pl.BlockSpec(memory_space=pltpu.VMEM)
SMEM = pl.BlockSpec(memory_space=pltpu.SMEM)
HBM = pl.BlockSpec(memory_space=pl.ANY)


def head_window(head):
    first = (head * HEAD_DIM) // 128 * 128
    offset = head * HEAD_DIM - first
    lane = lax.broadcasted_iota(jnp.int32, (1, WIN), 1)
    return first, (lane >= offset) & (lane < offset + HEAD_DIM)


def keep(lanes, values):
    return jnp.where(lanes, values, jnp.zeros_like(values))


def normalize(rows):
    values = rows.astype(F32)
    centered = values - jnp.mean(values, axis=-1, keepdims=True)
    inv_std = lax.rsqrt(jnp.mean(centered * centered, axis=-1, keepdims=True) + EPSILON)
    return centered * inv_std, inv_std


def pack_body(clip_ref, rows_ref, out_ref):
    out_ref[:, pl.ds(0, D)] = rows_ref[...]
    clip = jnp.full((ROWS, 128), clip_ref[0, 0], jnp.int32)
    out_ref[:, pl.ds(D, 128)] = clip.astype(F32).astype(BF)


def split_body(after_ref, rows_ref, *out_refs):
    me = lax.axis_index("seq")
    for k in range(SLOTS):
        start = pl.multiple_of((me ^ k) * CHUNK, CHUNK)
        out_refs[k][...] = rows_ref[pl.ds(start, CHUNK), :]


def join_body(*refs):
    out_ref = refs[SLOTS]
    me = lax.axis_index("seq")
    for k in range(SLOTS):
        start = pl.multiple_of((me ^ k) * CHUNK, CHUNK)
        out_ref[pl.ds(start, CHUNK), :] = refs[k][...]


def norm_body(x_ref, gain_ref, normed_ref):
    normalized, _ = normalize(x_ref[:, pl.ds(0, D)])
    normed_ref[...] = (normalized * gain_ref[...]).astype(BF)


def turn_body(normed_ref, mine_ref, theirs_ref, wide_ref, other_ref):
    core = lax.axis_index("seq") % 2
    for b in range(16):
        block = normed_ref[:, pl.ds(b * BLOCK // 128 * 128, 256 if b < 15 else 128)]
        offset = b * BLOCK % 128
        turned = jnp.transpose(block.astype(F32))[offset : offset + BLOCK]
        slot = lax.axis_index("dp") ^ b
        by_y = slot // 4 * 4 + b % 4
        by_z = slot % 4 * 4 + b // 4
        slot = jnp.where(core == 0, by_y, by_z)
        wide_ref[pl.ds(pl.multiple_of(slot * BLOCK, 8), BLOCK), :] = turned
        slot = jnp.where(core == 0, by_z, by_y)
        other_ref[pl.ds(pl.multiple_of(slot * BLOCK, 8), BLOCK), :] = turned
    mine_ref[...] = wide_ref[...].astype(BF)
    theirs_ref[...] = other_ref[...].astype(BF)


def project_body(x_ref, normed_ref, w_hbm, qkv_ref, soft_ref, prob_ref, wbuf, bias_ref, sems):
    first = [(0, 512), (512, 1152), (1664, 1152)]
    rest = [(2816, 384), (3200, 384), (3584, 384), (3968, 256)]

    def fetch(i, start, count):
        cols = pl.ds(start, count)
        return pltpu.make_async_copy(w_hbm.at[:, cols], wbuf.at[:, cols], sems.at[i])

    def project(i, start, count):
        cols = pl.ds(start, count)
        fetch(i, start, count).wait()
        out = jnp.dot(normed_ref[...], wbuf[:, cols], preferred_element_type=F32)
        qkv_ref[:, cols] = out.astype(BF)

    for i, (start, count) in enumerate(first + rest):
        fetch(i, start, count).start()

    row = lax.broadcasted_iota(jnp.int32, (ROWS, ROWS), 0)
    col = lax.broadcasted_iota(jnp.int32, (ROWS, ROWS), 1)
    clip = x_ref[:, pl.ds(D, 128)].astype(F32)
    clip = jnp.concatenate([clip, clip], axis=1)
    kept = (clip == jnp.transpose(clip)) & (row % CHUNK == col % CHUNK)
    bias_ref[...] = jnp.where(kept, 0.0, MASKED).astype(F32)
    qkv_ref[:, pl.ds(TRIPLE, 128)] = jnp.zeros((ROWS, 128), BF)

    for i, (start, count) in enumerate(first):
        project(i, start, count)

    def attend(head):
        start, lanes = head_window(head)
        query = qkv_ref[:, pl.ds(start, WIN)]
        key = keep(lanes, qkv_ref[:, pl.ds(D + start, WIN)])
        scores = lax.dot_general(key, query, (((1,), (1,)), ((), ())), preferred_element_type=F32)
        scores = scores * SCALING + bias_ref[...]
        powers = jnp.exp(scores - jnp.max(scores, axis=0, keepdims=True))
        softmaxed = powers / jnp.sum(powers, axis=0, keepdims=True)
        soft_ref[head] = softmaxed
        prob_ref[head] = softmaxed.astype(BF)

    qkv_ref[:, pl.ds(2 * D, 128)] = jnp.zeros((ROWS, 128), BF)
    for head in range(HEADS):
        attend(head)
        if head % 4 == 3:
            project(len(first) + head // 4, *rest[head // 4])


def value_body(prob_ref, *refs):
    chunks = refs[:SLOTS]
    dv_ref, mine_ref, theirs_ref, grad_ref, acc_ref = refs[SLOTS:]
    me = lax.axis_index("seq")
    for k in range(SLOTS):
        start = pl.multiple_of((me ^ k) * CHUNK, CHUNK)
        grad_ref[pl.ds(start, CHUNK), pl.ds(0, D)] = chunks[k][...]
    grad_ref[:, pl.ds(D, 128)] = jnp.zeros((ROWS, 128), BF)
    acc_ref[...] = jnp.zeros_like(acc_ref)

    def one(head):
        first, lanes = head_window(head)
        grad = keep(lanes, grad_ref[:, pl.ds(first, WIN)])
        acc_ref[:, pl.ds(first, WIN)] += jnp.dot(prob_ref[head], grad, preferred_element_type=F32)

    for head in range(HEADS):
        one(head)
    dv_ref[...] = acc_ref[:, pl.ds(0, D)].astype(BF)
    core = lax.axis_index("seq") % 2
    lead = D - HALF
    mine_ref[...] = dv_ref[:, pl.ds(pl.multiple_of(core * lead, 128), HALF)]
    theirs_ref[...] = dv_ref[:, pl.ds(pl.multiple_of((1 - core) * lead, 128), HALF)]


def weight_body(nt_ref, nt_other_ref, dv_ref, dv_other_ref, *out_refs):
    for tile in range(HALF // TILE):
        cols = pl.ds(tile * TILE, TILE)
        term = jnp.dot(nt_ref[...], dv_ref[:, cols], preferred_element_type=F32)
        term += jnp.dot(nt_other_ref[...], dv_other_ref[:, cols], preferred_element_type=F32)
        for j in range(4):
            out = out_refs[j]
            out[:, cols] = term[j * 4 * BLOCK : (j + 1) * 4 * BLOCK].astype(out.dtype)


def second_body(*refs):
    parts, gains, out_ref = refs[:4], refs[4:8], refs[8]
    gain = gains[0][...]
    for g in gains[1:]:
        gain = gain + g[...]
    gain = jnp.concatenate([gain, jnp.zeros((1, 2 * HALF - D), F32)], axis=1)
    rest = jnp.concatenate([gain[:, :HALF], gain[:, HALF:]], axis=0)
    total = parts[0][...]
    for part in parts[1:]:
        total = total + part[...].astype(F32)
    for i in range(16):
        rows = jnp.concatenate([total[i * 22 : i * 22 + 22], rest], axis=0)
        out_ref[i] = rows.astype(BF)


def third_body(parts_ref, mine_ref, theirs_ref):
    total = parts_ref[0].astype(F32)
    for i in range(1, 16):
        total = total + parts_ref[i].astype(F32)
    rest = jnp.concatenate([total[22:24], jnp.zeros((3, HALF), F32)], axis=0)
    low = jnp.concatenate([total[:11], rest], axis=0)
    high = jnp.concatenate([total[11:22], rest], axis=0)
    core = lax.axis_index("seq") % 2
    mine_ref[...] = jnp.where(core == 0, low, high)
    theirs_ref[...] = jnp.where(core == 0, high, low)


def last_body(factor):
    def body(mine_ref, other_ref, out_ref, gain_ref):
        core = lax.axis_index("seq") % 2
        mine, other = mine_ref[...] * factor, other_ref[...] * factor
        first = jnp.where(core == 0, mine, other)
        second = jnp.where(core == 0, other, mine)
        gain = (first + second)[11:13]
        out_ref[:, pl.ds(0, HALF)] = first[:11]
        out_ref[:, pl.ds(HALF, D - HALF)] = second[:11, 2 * HALF - D :]
        gain_ref[:, pl.ds(0, HALF)] = gain[0:1]
        gain_ref[:, pl.ds(HALF, D - HALF)] = gain[1:2, : D - HALF]

    return body


def input_body(*refs):
    x_ref, qkv_ref, soft_ref, grad_ref, dv_ref, gain_ref, w_hbm = refs[:7]
    outs, gain_out = refs[7 : 7 + SLOTS], refs[7 + SLOTS]
    wbuf, dq_ref, dk_ref, g_ref, dn_ref, sems = refs[8 + SLOTS :]
    tiles = [(0, 512), (512, 512), (1024, 384)]
    parts = [pl.ds(2 * D, D), pl.ds(0, 2 * D)]

    def fetch(part, i):
        at = pl.ds(*tiles[i]), parts[part]
        return pltpu.make_async_copy(w_hbm.at[at], wbuf.at[at], sems.at[part, i])

    for part in range(2):
        for i in range(len(tiles)):
            fetch(part, i).start()
    dq_ref[...] = jnp.zeros_like(dq_ref)
    dk_ref[...] = jnp.zeros_like(dk_ref)
    across = (((1,), (1,)), ((), ()))

    def one(head):
        first, lanes = head_window(head)
        query = keep(lanes, qkv_ref[:, pl.ds(first, WIN)])
        key = keep(lanes, qkv_ref[:, pl.ds(D + first, WIN)])
        value = keep(lanes, qkv_ref[:, pl.ds(2 * D + first, WIN)])
        grad = grad_ref[:, pl.ds(first, WIN)]
        d_probs = lax.dot_general(value, grad, across, preferred_element_type=F32)
        softmaxed = soft_ref[head]
        row_dot = jnp.sum(softmaxed * d_probs, axis=0, keepdims=True)
        d_scores = (softmaxed * (d_probs - row_dot) * SCALING).astype(BF)
        dk_ref[:, pl.ds(first, WIN)] += jnp.dot(d_scores, query, preferred_element_type=F32)
        dq_ref[:, pl.ds(first, WIN)] += lax.dot_general(
            d_scores, key, (((0,), (0,)), ((), ())), preferred_element_type=F32
        )

    for head in range(HEADS):
        one(head)
        if head % 4 == 3 and head < 15:
            i = head // 4
            fetch(0, i).wait()
            rows = pl.ds(*tiles[i])
            dn_ref[:, rows] = lax.dot_general(
                dv_ref[...], wbuf[rows, parts[0]], across, preferred_element_type=F32
            )
    g_ref[:, pl.ds(0, D)] = dq_ref[:, pl.ds(0, D)].astype(BF)
    g_ref[:, pl.ds(D, D)] = dk_ref[:, pl.ds(0, D)].astype(BF)
    for i in range(len(tiles)):
        fetch(1, i).wait()
        rows = pl.ds(*tiles[i])
        dn_ref[:, rows] += lax.dot_general(
            g_ref[...], wbuf[rows, parts[1]], across, preferred_element_type=F32
        )
    gain = gain_ref[...]
    gain_sum = jnp.zeros((1, D), F32)
    me = lax.axis_index("seq")
    for k in range(SLOTS):
        rows = pl.ds(pl.multiple_of((me ^ k) * CHUNK, CHUNK), CHUNK)
        normalized, inv_std = normalize(x_ref[rows, pl.ds(0, D)])
        d_normed = dn_ref[rows, :]
        gain_sum = gain_sum + jnp.sum(d_normed * normalized, axis=0, keepdims=True)
        d_hat = d_normed * gain
        first_mean = jnp.mean(d_hat, axis=-1, keepdims=True)
        second_mean = jnp.mean(d_hat * normalized, axis=-1, keepdims=True)
        out = inv_std * (d_hat - first_mean - normalized * second_mean)
        outs[k][...] = out.astype(BF)
    gain_out[...] = gain_sum


def swap_seq(value, k):
    return lax.ppermute(value, "seq", [(i, i ^ k) for i in range(SLOTS)])


def swap_plane(value, j):
    pairs = []
    for dp in range(16):
        for seq in range(SLOTS):
            pairs.append((dp * SLOTS + seq, (dp ^ (4 * j if seq % 2 == 0 else j)) * SLOTS + seq))
    return lax.ppermute(value, ("dp", "seq"), pairs)


def exchange_plane(blocks):
    groups = []
    for core in range(2):
        for i in range(4):
            plane = [4 * i + j if core == 0 else 4 * j + i for j in range(4)]
            groups.append([dp * SLOTS + 2 * x + core for dp in plane for x in range(4)])
    return lax.all_to_all(
        blocks, ("dp", "seq"), split_axis=0, concat_axis=0, tiled=True, axis_index_groups=groups
    )


def exchange(rows):
    blocks = rows.reshape(SLOTS, CHUNK, -1)
    moved = lax.all_to_all(blocks, "seq", split_axis=0, concat_axis=0, tiled=True)
    return moved.reshape(rows.shape)


def four(rank, dims):
    return [shape(dims, F32)] + [shape(dims, BF)] * (rank - 1)


def shards(block_input, norm_gain, qkv_weight, frame_clip, out_grad):
    factor = 32768 ** (-0.5)
    gain = norm_gain.reshape(1, D)

    packed = call(
        pack_body,
        shape((ROWS, WIDE), BF),
        in_specs=[SMEM, VMEM],
        mib=8,
        data=10**6,
        name="pack",
    )(frame_clip, block_input.reshape(ROWS, D))
    x = exchange(packed)
    chunks = [shape((CHUNK, D), BF)] * SLOTS
    sent = call(
        split_body, chunks, in_specs=[pl.BlockSpec(memory_space=pl.ANY), VMEM], mib=8, data=10**6, name="split"
    )(x, out_grad.reshape(ROWS, D))
    grads = [sent[0]] + [swap_seq(sent[k], k) for k in range(1, SLOTS)]

    normed = call(norm_body, shape((ROWS, D), BF), mib=8, data=10**6, name="norm")(x, gain)
    nt, nt_sent = call(
        turn_body,
        [shape((D, ROWS), BF)] * 2,
        scratch=[pltpu.VMEM((D, ROWS), F32)] * 2,
        mib=8,
        data=4 * 10**6,
        name="turn",
    )(normed)
    nt_other = swap_seq(nt_sent, 1)
    qkv, soft, probs = call(
        project_body,
        [
            shape((ROWS, PADDED), BF),
            shape((HEADS, ROWS, ROWS), F32),
            shape((HEADS, ROWS, ROWS), BF),
        ],
        scratch=[
            pltpu.VMEM((D, TRIPLE), BF),
            pltpu.VMEM((ROWS, ROWS), F32),
            pltpu.SemaphoreType.DMA((7,)),
        ],
        in_specs=[VMEM, VMEM, HBM],
        mib=40,
        flops=5 * 10**9,
        data=40 * 10**6,
        name="project",
    )(x, normed, qkv_weight)

    d_value, mine, theirs, grad_wide = call(
        value_body,
        [
            shape((ROWS, D), BF),
            shape((ROWS, HALF), BF),
            shape((ROWS, HALF), BF),
            shape((ROWS, WIDE), BF),
        ],
        scratch=[pltpu.VMEM((ROWS, WIDE), F32)],
        mib=16,
        flops=10**9,
        data=5 * 10**6,
        name="value",
    )(probs, *grads)
    other = swap_seq(theirs, 1)
    terms = call(
        weight_body,
        four(4, (4 * BLOCK, HALF)),
        mib=16,
        flops=11 * 10**8,
        data=6 * 10**6,
        name="weight",
    )(nt, nt_other, mine, other)
    terms = [terms[0]] + [swap_plane(terms[j], j) for j in range(1, 4)]

    results = call(
        input_body,
        chunks + [shape((1, D), F32)],
        scratch=[
            pltpu.VMEM((D, TRIPLE), BF),
            pltpu.VMEM((ROWS, WIDE), F32),
            pltpu.VMEM((ROWS, WIDE), F32),
            pltpu.VMEM((ROWS, 2 * D), BF),
            pltpu.VMEM((ROWS, D), F32),
            pltpu.SemaphoreType.DMA((2, 3)),
        ],
        in_specs=[VMEM] * 6 + [HBM],
        mib=40,
        flops=6 * 10**9,
        data=20 * 10**6,
        name="input",
    )(x, qkv, soft, grad_wide, d_value, gain, qkv_weight)
    returned = [results[0]] + [swap_seq(results[k], k) for k in range(1, SLOTS)]
    gain_term = results[SLOTS]
    gains = [gain_term] + [swap_plane(gain_term, j) for j in range(1, 4)]

    sums = call(second_body, shape((16, 24, HALF), BF), mib=16, data=5 * 10**6, name="second")(
        *terms, *gains
    )
    sums = exchange_plane(sums)
    mine, theirs = call(third_body, [shape((16, HALF), F32)] * 2, mib=8, data=10**6, name="third")(
        sums
    )
    weight_grad, gain_grad = call(
        last_body(factor),
        [shape((11, D), F32), shape((1, D), F32)],
        mib=8,
        data=10**5,
        name="last",
    )(mine, swap_seq(theirs, 1))
    input_grad = call(join_body, shape((ROWS, D), BF), mib=8, data=10**6, name="join")(*returned)
    return input_grad.reshape(block_input.shape), weight_grad, gain_grad.reshape(D)


def solution(mesh):
    placed = (P("dp", "seq", None, None), P(), P(), P("dp", "seq"), P("dp", "seq", None, None))
    return jax.shard_map(
        shards,
        mesh=mesh,
        in_specs=placed,
        out_specs=(P("dp", "seq", None, None), P(("dp", "seq"), None), P()),
        check_vma=False,
    )
```

```python
import jax
import jax.numpy as jnp
from jax import lax
from jax.experimental import pallas as pl
from jax.experimental.pallas import tpu as pltpu
from jax.sharding import PartitionSpec as P

HEADS = 16
HEAD_DIM = 88
D = 1408
TRIPLE = 3 * D
WIN = 256
PADDED = TRIPLE + 128
WIDE = D + 128
ROWS = 256
CHUNK = 32
SLOTS = 8
CHIPS = 4
PAIR = 2 * CHUNK
TILE = 256
BLOCK = 88
HALF = 768
EPSILON = 1e-06
SCALING = HEAD_DIM ** (-0.5)
MASKED = -1e30

BF = jnp.bfloat16
F32 = jnp.float32


def shape(dims, dtype):
    return jax.ShapeDtypeStruct(dims, dtype)


def call(body, outs, scratch=(), in_specs=None, mib=16, flops=0, data=0, name=None):
    extra = {} if in_specs is None else {"in_specs": in_specs}
    return pl.pallas_call(
        body,
        out_shape=outs,
        scratch_shapes=list(scratch),
        compiler_params=pltpu.CompilerParams(vmem_limit_bytes=mib << 20),
        cost_estimate=pl.CostEstimate(flops=flops, bytes_accessed=data, transcendentals=0),
        name=name,
        **extra,
    )


VMEM = pl.BlockSpec(memory_space=pltpu.VMEM)
SMEM = pl.BlockSpec(memory_space=pltpu.SMEM)
HBM = pl.BlockSpec(memory_space=pl.ANY)


def head_window(head):
    first = (head * HEAD_DIM) // 128 * 128
    offset = head * HEAD_DIM - first
    lane = lax.broadcasted_iota(jnp.int32, (1, WIN), 1)
    return first, (lane >= offset) & (lane < offset + HEAD_DIM)


def keep(lanes, values):
    return jnp.where(lanes, values, jnp.zeros_like(values))


def normalize(rows):
    values = rows.astype(F32)
    centered = values - jnp.mean(values, axis=-1, keepdims=True)
    inv_std = lax.rsqrt(jnp.mean(centered * centered, axis=-1, keepdims=True) + EPSILON)
    return centered * inv_std, inv_std


def place():
    me = lax.axis_index("seq")
    return me // 2, me % 2


def part_rows(chip, core):
    return pl.ds(pl.multiple_of((2 * chip + core) * CHUNK, CHUNK), CHUNK)


def split_body(rows_ref, *refs):
    clip_ref, (mine_ref, theirs_ref) = refs[:-2], refs[-2:]
    chip, core = place()
    for j in range(CHIPS):
        mine_ref[j, :, pl.ds(0, D)] = rows_ref[part_rows(chip ^ j, core), :]
        theirs_ref[j, :, pl.ds(0, D)] = rows_ref[part_rows(chip ^ j, 1 - core), :]
    if clip_ref:
        clip = jnp.full((CHIPS, CHUNK, 128), clip_ref[0][0, 0], jnp.int32).astype(F32).astype(BF)
        mine_ref[:, :, pl.ds(D, 128)] = clip
        theirs_ref[:, :, pl.ds(D, 128)] = clip


def merge_body(mine_ref, other_ref, *refs):
    out_refs = refs[-CHIPS:]
    _, core = place()
    for j in range(CHIPS):
        out_refs[j][pl.ds(pl.multiple_of(core * CHUNK, CHUNK), CHUNK), :] = mine_ref[j]
        out_refs[j][pl.ds(pl.multiple_of((1 - core) * CHUNK, CHUNK), CHUNK), :] = other_ref[j]


def part_body(*refs):
    mine_ref, theirs_ref = refs[CHIPS:]
    _, core = place()
    for j in range(CHIPS):
        mine_ref[j] = refs[j][pl.ds(pl.multiple_of(core * CHUNK, CHUNK), CHUNK), :]
        theirs_ref[j] = refs[j][pl.ds(pl.multiple_of((1 - core) * CHUNK, CHUNK), CHUNK), :]


def join_body(mine_ref, other_ref, out_ref):
    chip, core = place()
    for j in range(CHIPS):
        out_ref[part_rows(chip ^ j, core), :] = mine_ref[j]
        out_ref[part_rows(chip ^ j, 1 - core), :] = other_ref[j]


def norm_body(*refs):
    xs, (gain_ref, normed_ref, clip_ref) = refs[:CHIPS], refs[CHIPS:]
    for j in range(CHIPS):
        rows = pl.ds(j * PAIR, PAIR)
        normalized, _ = normalize(xs[j][:, pl.ds(0, D)])
        normed_ref[rows, :] = (normalized * gain_ref[...]).astype(BF)
        clip_ref[rows, :] = xs[j][:, pl.ds(D, 128)].astype(F32)


def turn_body(normed_ref, mine_ref, theirs_ref, wide_ref, other_ref):
    core = lax.axis_index("seq") % 2
    for b in range(16):
        block = normed_ref[:, pl.ds(b * BLOCK // 128 * 128, 256 if b < 15 else 128)]
        offset = b * BLOCK % 128
        turned = jnp.transpose(block.astype(F32))[offset : offset + BLOCK]
        slot = lax.axis_index("dp") ^ b
        by_y = slot // 4 * 4 + b % 4
        by_z = slot % 4 * 4 + b // 4
        slot = jnp.where(core == 0, by_y, by_z)
        wide_ref[pl.ds(pl.multiple_of(slot * BLOCK, 8), BLOCK), :] = turned
        slot = jnp.where(core == 0, by_z, by_y)
        other_ref[pl.ds(pl.multiple_of(slot * BLOCK, 8), BLOCK), :] = turned
    mine_ref[...] = wide_ref[...].astype(BF)
    theirs_ref[...] = other_ref[...].astype(BF)


def project_body(clip_ref, normed_ref, w_hbm, qkv_ref, soft_ref, prob_ref, wbuf, bias_ref, sems):
    first = [(0, 512), (512, 1152), (1664, 1152)]
    rest = [(2816, 384), (3200, 384), (3584, 384), (3968, 256)]

    def fetch(i, start, count):
        cols = pl.ds(start, count)
        return pltpu.make_async_copy(w_hbm.at[:, cols], wbuf.at[:, cols], sems.at[i])

    def project(i, start, count):
        cols = pl.ds(start, count)
        fetch(i, start, count).wait()
        out = jnp.dot(normed_ref[...], wbuf[:, cols], preferred_element_type=F32)
        qkv_ref[:, cols] = out.astype(BF)

    for i, (start, count) in enumerate(first + rest):
        fetch(i, start, count).start()

    row = lax.broadcasted_iota(jnp.int32, (ROWS, ROWS), 0)
    col = lax.broadcasted_iota(jnp.int32, (ROWS, ROWS), 1)
    clip = clip_ref[...]
    clip = jnp.concatenate([clip, clip], axis=1)
    kept = (clip == jnp.transpose(clip)) & (row % CHUNK == col % CHUNK)
    bias_ref[...] = jnp.where(kept, 0.0, MASKED).astype(F32)
    qkv_ref[:, pl.ds(TRIPLE, 128)] = jnp.zeros((ROWS, 128), BF)

    for i, (start, count) in enumerate(first):
        project(i, start, count)

    def attend(head):
        start, lanes = head_window(head)
        query = qkv_ref[:, pl.ds(start, WIN)]
        key = keep(lanes, qkv_ref[:, pl.ds(D + start, WIN)])
        scores = lax.dot_general(key, query, (((1,), (1,)), ((), ())), preferred_element_type=F32)
        scores = scores * SCALING + bias_ref[...]
        powers = jnp.exp(scores - jnp.max(scores, axis=0, keepdims=True))
        softmaxed = powers / jnp.sum(powers, axis=0, keepdims=True)
        soft_ref[head] = softmaxed
        prob_ref[head] = softmaxed.astype(BF)

    qkv_ref[:, pl.ds(2 * D, 128)] = jnp.zeros((ROWS, 128), BF)
    for head in range(HEADS):
        attend(head)
        if head % 4 == 3:
            project(len(first) + head // 4, *rest[head // 4])


def value_body(prob_ref, *refs):
    chunks = refs[:CHIPS]
    dv_ref, mine_ref, theirs_ref, grad_ref, acc_ref = refs[CHIPS:]
    for j in range(CHIPS):
        grad_ref[pl.ds(j * PAIR, PAIR), pl.ds(0, D)] = chunks[j][...]
    grad_ref[:, pl.ds(D, 128)] = jnp.zeros((ROWS, 128), BF)
    acc_ref[...] = jnp.zeros_like(acc_ref)

    def one(head):
        first, lanes = head_window(head)
        grad = keep(lanes, grad_ref[:, pl.ds(first, WIN)])
        acc_ref[:, pl.ds(first, WIN)] += jnp.dot(prob_ref[head], grad, preferred_element_type=F32)

    for head in range(HEADS):
        one(head)
    dv_ref[...] = acc_ref[:, pl.ds(0, D)].astype(BF)
    core = lax.axis_index("seq") % 2
    lead = D - HALF
    mine_ref[...] = dv_ref[:, pl.ds(pl.multiple_of(core * lead, 128), HALF)]
    theirs_ref[...] = dv_ref[:, pl.ds(pl.multiple_of((1 - core) * lead, 128), HALF)]


def weight_body(nt_ref, nt_other_ref, dv_ref, dv_other_ref, *out_refs):
    for tile in range(HALF // TILE):
        cols = pl.ds(tile * TILE, TILE)
        term = jnp.dot(nt_ref[...], dv_ref[:, cols], preferred_element_type=F32)
        term += jnp.dot(nt_other_ref[...], dv_other_ref[:, cols], preferred_element_type=F32)
        for j in range(4):
            out = out_refs[j]
            out[:, cols] = term[j * 4 * BLOCK : (j + 1) * 4 * BLOCK].astype(out.dtype)


def second_body(*refs):
    parts, gains, out_ref = refs[:4], refs[4:8], refs[8]
    gain = gains[0][...]
    for g in gains[1:]:
        gain = gain + g[...]
    gain = jnp.concatenate([gain, jnp.zeros((1, 2 * HALF - D), F32)], axis=1)
    rest = jnp.concatenate([gain[:, :HALF], gain[:, HALF:]], axis=0)
    total = parts[0][...]
    for part in parts[1:]:
        total = total + part[...].astype(F32)
    for i in range(16):
        rows = jnp.concatenate([total[i * 22 : i * 22 + 22], rest], axis=0)
        out_ref[i] = rows.astype(BF)


def third_body(parts_ref, mine_ref, theirs_ref):
    total = parts_ref[0].astype(F32)
    for i in range(1, 16):
        total = total + parts_ref[i].astype(F32)
    rest = jnp.concatenate([total[22:24], jnp.zeros((3, HALF), F32)], axis=0)
    low = jnp.concatenate([total[:11], rest], axis=0)
    high = jnp.concatenate([total[11:22], rest], axis=0)
    core = lax.axis_index("seq") % 2
    mine_ref[...] = jnp.where(core == 0, low, high)
    theirs_ref[...] = jnp.where(core == 0, high, low)


def last_body(factor):
    def body(mine_ref, other_ref, out_ref, gain_ref):
        core = lax.axis_index("seq") % 2
        mine, other = mine_ref[...] * factor, other_ref[...] * factor
        first = jnp.where(core == 0, mine, other)
        second = jnp.where(core == 0, other, mine)
        gain = (first + second)[11:13]
        out_ref[:, pl.ds(0, HALF)] = first[:11]
        out_ref[:, pl.ds(HALF, D - HALF)] = second[:11, 2 * HALF - D :]
        gain_ref[:, pl.ds(0, HALF)] = gain[0:1]
        gain_ref[:, pl.ds(HALF, D - HALF)] = gain[1:2, : D - HALF]

    return body


def input_body(*refs):
    xs, refs = refs[:CHIPS], refs[CHIPS:]
    qkv_ref, soft_ref, grad_ref, dv_ref, gain_ref, w_hbm = refs[:6]
    outs, gain_out = refs[6 : 6 + CHIPS], refs[6 + CHIPS]
    wbuf, dq_ref, dk_ref, g_ref, dn_ref, sems = refs[7 + CHIPS :]
    tiles = [(0, 512), (512, 512), (1024, 384)]
    parts = [pl.ds(2 * D, D), pl.ds(0, 2 * D)]

    def fetch(part, i):
        at = pl.ds(*tiles[i]), parts[part]
        return pltpu.make_async_copy(w_hbm.at[at], wbuf.at[at], sems.at[part, i])

    for part in range(2):
        for i in range(len(tiles)):
            fetch(part, i).start()
    dq_ref[...] = jnp.zeros_like(dq_ref)
    dk_ref[...] = jnp.zeros_like(dk_ref)
    across = (((1,), (1,)), ((), ()))

    def one(head):
        first, lanes = head_window(head)
        query = keep(lanes, qkv_ref[:, pl.ds(first, WIN)])
        key = keep(lanes, qkv_ref[:, pl.ds(D + first, WIN)])
        value = keep(lanes, qkv_ref[:, pl.ds(2 * D + first, WIN)])
        grad = grad_ref[:, pl.ds(first, WIN)]
        d_probs = lax.dot_general(value, grad, across, preferred_element_type=F32)
        softmaxed = soft_ref[head]
        row_dot = jnp.sum(softmaxed * d_probs, axis=0, keepdims=True)
        d_scores = (softmaxed * (d_probs - row_dot) * SCALING).astype(BF)
        dk_ref[:, pl.ds(first, WIN)] += jnp.dot(d_scores, query, preferred_element_type=F32)
        dq_ref[:, pl.ds(first, WIN)] += lax.dot_general(
            d_scores, key, (((0,), (0,)), ((), ())), preferred_element_type=F32
        )

    for head in range(HEADS):
        one(head)
        if head % 4 == 3 and head < 15:
            i = head // 4
            fetch(0, i).wait()
            rows = pl.ds(*tiles[i])
            dn_ref[:, rows] = lax.dot_general(
                dv_ref[...], wbuf[rows, parts[0]], across, preferred_element_type=F32
            )
    g_ref[:, pl.ds(0, D)] = dq_ref[:, pl.ds(0, D)].astype(BF)
    g_ref[:, pl.ds(D, D)] = dk_ref[:, pl.ds(0, D)].astype(BF)
    for i in range(len(tiles)):
        fetch(1, i).wait()
        rows = pl.ds(*tiles[i])
        dn_ref[:, rows] += lax.dot_general(
            g_ref[...], wbuf[rows, parts[1]], across, preferred_element_type=F32
        )
    gain = gain_ref[...]
    gain_sum = jnp.zeros((1, D), F32)
    for k in range(SLOTS):
        rows = pl.ds(k % 2 * CHUNK, CHUNK)
        normalized, inv_std = normalize(xs[k // 2][rows, pl.ds(0, D)])
        d_normed = dn_ref[pl.ds(k * CHUNK, CHUNK), :]
        gain_sum = gain_sum + jnp.sum(d_normed * normalized, axis=0, keepdims=True)
        d_hat = d_normed * gain
        first_mean = jnp.mean(d_hat, axis=-1, keepdims=True)
        second_mean = jnp.mean(d_hat * normalized, axis=-1, keepdims=True)
        out = inv_std * (d_hat - first_mean - normalized * second_mean)
        outs[k // 2][rows, :] = out.astype(BF)
    gain_out[...] = gain_sum


def swap_seq(value, k):
    return lax.ppermute(value, "seq", [(i, i ^ k) for i in range(SLOTS)])


def swap_plane(value, j):
    pairs = []
    for dp in range(16):
        for seq in range(SLOTS):
            pairs.append((dp * SLOTS + seq, (dp ^ (4 * j if seq % 2 == 0 else j)) * SLOTS + seq))
    return lax.ppermute(value, ("dp", "seq"), pairs)


def exchange_plane(blocks):
    groups = []
    for core in range(2):
        for i in range(4):
            plane = [4 * i + j if core == 0 else 4 * j + i for j in range(4)]
            groups.append([dp * SLOTS + 2 * x + core for dp in plane for x in range(4)])
    return lax.all_to_all(
        blocks, ("dp", "seq"), split_axis=0, concat_axis=0, tiled=True, axis_index_groups=groups
    )


def swap_chips(chunks):
    return [chunks[0]] + [swap_seq(chunks[j], 2 * j) for j in range(1, CHIPS)]


def spread(rows, *clip, after=()):
    width = D + 128 * len(clip)
    mine, theirs = call(
        split_body,
        [shape((CHIPS, CHUNK, width), BF)] * 2,
        in_specs=[VMEM] + [SMEM] * len(clip),
        mib=8,
        data=10**6,
        name="split",
    )(rows, *clip)
    chunks = call(
        merge_body,
        [shape((PAIR, width), BF)] * CHIPS,
        in_specs=[VMEM, VMEM] + [pl.BlockSpec(memory_space=pl.ANY)] * len(after),
        mib=8,
        data=10**6,
        name="merge",
    )(mine, swap_seq(theirs, 1), *after)
    return swap_chips(chunks)


def gather(chunks):
    mine, theirs = call(
        part_body,
        [shape((CHIPS, CHUNK, D), BF)] * 2,
        mib=8,
        flops=2 * 10**10,
        data=10**6,
        name="part",
    )(*swap_chips(chunks))
    return call(join_body, shape((ROWS, D), BF), mib=8, data=10**6, name="join")(
        mine, swap_seq(theirs, 1)
    )


def four(rank, dims):
    return [shape(dims, F32)] + [shape(dims, BF)] * (rank - 1)


def shards(block_input, norm_gain, qkv_weight, frame_clip, out_grad):
    factor = 32768 ** (-0.5)
    gain = norm_gain.reshape(1, D)

    x = spread(block_input.reshape(ROWS, D), frame_clip)
    grads = spread(out_grad.reshape(ROWS, D), after=x[1:2])

    normed, clips = call(
        norm_body, [shape((ROWS, D), BF), shape((ROWS, 128), F32)], mib=8, data=10**6, name="norm"
    )(*x, gain)
    nt, nt_sent = call(
        turn_body,
        [shape((D, ROWS), BF)] * 2,
        scratch=[pltpu.VMEM((D, ROWS), F32)] * 2,
        mib=8,
        data=4 * 10**6,
        name="turn",
    )(normed)
    nt_other = swap_seq(nt_sent, 1)
    qkv, soft, probs = call(
        project_body,
        [
            shape((ROWS, PADDED), BF),
            shape((HEADS, ROWS, ROWS), F32),
            shape((HEADS, ROWS, ROWS), BF),
        ],
        scratch=[
            pltpu.VMEM((D, TRIPLE), BF),
            pltpu.VMEM((ROWS, ROWS), F32),
            pltpu.SemaphoreType.DMA((7,)),
        ],
        in_specs=[VMEM, VMEM, HBM],
        mib=40,
        flops=5 * 10**9,
        data=40 * 10**6,
        name="project",
    )(clips, normed, qkv_weight)

    d_value, mine, theirs, grad_wide = call(
        value_body,
        [
            shape((ROWS, D), BF),
            shape((ROWS, HALF), BF),
            shape((ROWS, HALF), BF),
            shape((ROWS, WIDE), BF),
        ],
        scratch=[pltpu.VMEM((ROWS, WIDE), F32)],
        mib=16,
        flops=10**9,
        data=5 * 10**6,
        name="value",
    )(probs, *grads)
    other = swap_seq(theirs, 1)
    terms = call(
        weight_body,
        four(4, (4 * BLOCK, HALF)),
        mib=16,
        flops=11 * 10**8,
        data=6 * 10**6,
        name="weight",
    )(nt, nt_other, mine, other)
    terms = [terms[0]] + [swap_plane(terms[j], j) for j in range(1, 4)]

    results = call(
        input_body,
        [shape((PAIR, D), BF)] * CHIPS + [shape((1, D), F32)],
        scratch=[
            pltpu.VMEM((D, TRIPLE), BF),
            pltpu.VMEM((ROWS, WIDE), F32),
            pltpu.VMEM((ROWS, WIDE), F32),
            pltpu.VMEM((ROWS, 2 * D), BF),
            pltpu.VMEM((ROWS, D), F32),
            pltpu.SemaphoreType.DMA((2, 3)),
        ],
        in_specs=[VMEM] * (CHIPS + 5) + [HBM],
        mib=40,
        flops=6 * 10**9,
        data=20 * 10**6,
        name="input",
    )(*x, qkv, soft, grad_wide, d_value, gain, qkv_weight)
    returned, gain_term = results[:CHIPS], results[CHIPS]
    gains = [gain_term] + [swap_plane(gain_term, j) for j in range(1, 4)]

    sums = call(second_body, shape((16, 24, HALF), BF), mib=16, data=5 * 10**6, name="second")(
        *terms, *gains
    )
    sums = exchange_plane(sums)
    mine, theirs = call(third_body, [shape((16, HALF), F32)] * 2, mib=8, data=10**6, name="third")(
        sums
    )
    weight_grad, gain_grad = call(
        last_body(factor),
        [shape((11, D), F32), shape((1, D), F32)],
        mib=8,
        data=10**5,
        name="last",
    )(mine, swap_seq(theirs, 1))
    input_grad = gather(returned)
    return input_grad.reshape(block_input.shape), weight_grad, gain_grad.reshape(D)


def solution(mesh):
    placed = (P("dp", "seq", None, None), P(), P(), P("dp", "seq"), P("dp", "seq", None, None))
    return jax.shard_map(
        shards,
        mesh=mesh,
        in_specs=placed,
        out_specs=(P("dp", "seq", None, None), P(("dp", "seq"), None), P()),
        check_vma=False,
    )
```

```python
import jax
import jax.numpy as jnp
from jax import lax
from jax.experimental import pallas as pl
from jax.experimental.pallas import tpu as pltpu
from jax.sharding import PartitionSpec as P

HEADS = 16
HEAD_DIM = 88
D = 1408
TRIPLE = 3 * D
WIN = 256
PADDED = TRIPLE + 128
WIDE = D + 128
ROWS = 256
CHUNK = 32
SLOTS = 8
CHIPS = 4
PAIR = 2 * CHUNK
TILE = 256
BLOCK = 88
HALF = 768
EPSILON = 1e-06
SCALING = HEAD_DIM ** (-0.5)
MASKED = -1e30

BF = jnp.bfloat16
F32 = jnp.float32


def shape(dims, dtype):
    return jax.ShapeDtypeStruct(dims, dtype)


def call(body, outs, scratch=(), in_specs=None, mib=16, flops=0, data=0, name=None):
    extra = {} if in_specs is None else {"in_specs": in_specs}
    return pl.pallas_call(
        body,
        out_shape=outs,
        scratch_shapes=list(scratch),
        compiler_params=pltpu.CompilerParams(vmem_limit_bytes=mib << 20),
        cost_estimate=pl.CostEstimate(flops=flops, bytes_accessed=data, transcendentals=0),
        name=name,
        **extra,
    )


VMEM = pl.BlockSpec(memory_space=pltpu.VMEM)
SMEM = pl.BlockSpec(memory_space=pltpu.SMEM)
HBM = pl.BlockSpec(memory_space=pl.ANY)


def head_window(head):
    first = (head * HEAD_DIM) // 128 * 128
    offset = head * HEAD_DIM - first
    lane = lax.broadcasted_iota(jnp.int32, (1, WIN), 1)
    return first, (lane >= offset) & (lane < offset + HEAD_DIM)


def keep(lanes, values):
    return jnp.where(lanes, values, jnp.zeros_like(values))


def normalize(rows):
    values = rows.astype(F32)
    centered = values - jnp.mean(values, axis=-1, keepdims=True)
    inv_std = lax.rsqrt(jnp.mean(centered * centered, axis=-1, keepdims=True) + EPSILON)
    return centered * inv_std, inv_std


def place():
    me = lax.axis_index("seq")
    return me // 2, me % 2


def part_rows(chip, core):
    return pl.ds(pl.multiple_of((2 * chip + core) * CHUNK, CHUNK), CHUNK)


def split_body(rows_ref, *refs):
    clip_ref, (mine_ref, theirs_ref) = refs[:-2], refs[-2:]
    chip, core = place()
    for j in range(CHIPS):
        mine_ref[j, :, pl.ds(0, D)] = rows_ref[part_rows(chip ^ j, core), :]
        theirs_ref[j, :, pl.ds(0, D)] = rows_ref[part_rows(chip ^ j, 1 - core), :]
    if clip_ref:
        clip = jnp.full((CHIPS, CHUNK, 128), clip_ref[0][0, 0], jnp.int32).astype(F32).astype(BF)
        mine_ref[:, :, pl.ds(D, 128)] = clip
        theirs_ref[:, :, pl.ds(D, 128)] = clip


def merge_body(mine_ref, other_ref, *refs):
    out_refs = refs[-CHIPS:]
    _, core = place()
    for j in range(CHIPS):
        out_refs[j][pl.ds(pl.multiple_of(core * CHUNK, CHUNK), CHUNK), :] = mine_ref[j]
        out_refs[j][pl.ds(pl.multiple_of((1 - core) * CHUNK, CHUNK), CHUNK), :] = other_ref[j]


def part_body(*refs):
    mine_ref, theirs_ref = refs[CHIPS:]
    _, core = place()
    for j in range(CHIPS):
        mine_ref[j] = refs[j][pl.ds(pl.multiple_of(core * CHUNK, CHUNK), CHUNK), :]
        theirs_ref[j] = refs[j][pl.ds(pl.multiple_of((1 - core) * CHUNK, CHUNK), CHUNK), :]


def join_body(mine_ref, other_ref, out_ref):
    chip, core = place()
    for j in range(CHIPS):
        out_ref[part_rows(chip ^ j, core), :] = mine_ref[j]
        out_ref[part_rows(chip ^ j, 1 - core), :] = other_ref[j]


def load_body(w_hbm, w_ref, sem):
    copy = pltpu.make_async_copy(w_hbm, w_ref, sem)
    copy.start()
    copy.wait()


def norm_body(*refs):
    xs, (gain_ref, _, normed_ref, clip_ref) = refs[:CHIPS], refs[CHIPS:]
    for j in range(CHIPS):
        rows = pl.ds(j * PAIR, PAIR)
        normalized, _ = normalize(xs[j][:, pl.ds(0, D)])
        normed_ref[rows, :] = (normalized * gain_ref[...]).astype(BF)
        clip_ref[rows, :] = xs[j][:, pl.ds(D, 128)].astype(F32)


def turn_body(normed_ref, mine_ref, theirs_ref, wide_ref, other_ref):
    core = lax.axis_index("seq") % 2
    for b in range(16):
        block = normed_ref[:, pl.ds(b * BLOCK // 128 * 128, 256 if b < 15 else 128)]
        offset = b * BLOCK % 128
        turned = jnp.transpose(block.astype(F32))[offset : offset + BLOCK]
        slot = lax.axis_index("dp") ^ b
        by_y = slot // 4 * 4 + b % 4
        by_z = slot % 4 * 4 + b // 4
        slot = jnp.where(core == 0, by_y, by_z)
        wide_ref[pl.ds(pl.multiple_of(slot * BLOCK, 8), BLOCK), :] = turned
        slot = jnp.where(core == 0, by_z, by_y)
        other_ref[pl.ds(pl.multiple_of(slot * BLOCK, 8), BLOCK), :] = turned
    mine_ref[...] = wide_ref[...].astype(BF)
    theirs_ref[...] = other_ref[...].astype(BF)


def project_body(clip_ref, normed_ref, wbuf, qkv_ref, soft_ref, prob_ref, bias_ref):
    first = [(0, 512), (512, 1152), (1664, 1152)]
    rest = [(2816, 384), (3200, 384), (3584, 384), (3968, 256)]

    def project(start, count):
        cols = pl.ds(start, count)
        out = jnp.dot(normed_ref[...], wbuf[:, cols], preferred_element_type=F32)
        qkv_ref[:, cols] = out.astype(BF)

    row = lax.broadcasted_iota(jnp.int32, (ROWS, ROWS), 0)
    col = lax.broadcasted_iota(jnp.int32, (ROWS, ROWS), 1)
    clip = clip_ref[...]
    clip = jnp.concatenate([clip, clip], axis=1)
    kept = (clip == jnp.transpose(clip)) & (row % CHUNK == col % CHUNK)
    bias_ref[...] = jnp.where(kept, 0.0, MASKED).astype(F32)
    qkv_ref[:, pl.ds(TRIPLE, 128)] = jnp.zeros((ROWS, 128), BF)

    for start, count in first:
        project(start, count)

    def attend(head):
        start, lanes = head_window(head)
        query = qkv_ref[:, pl.ds(start, WIN)]
        key = keep(lanes, qkv_ref[:, pl.ds(D + start, WIN)])
        scores = lax.dot_general(key, query, (((1,), (1,)), ((), ())), preferred_element_type=F32)
        scores = scores * SCALING + bias_ref[...]
        powers = jnp.exp(scores - jnp.max(scores, axis=0, keepdims=True))
        softmaxed = powers / jnp.sum(powers, axis=0, keepdims=True)
        soft_ref[head] = softmaxed
        prob_ref[head] = softmaxed.astype(BF)

    qkv_ref[:, pl.ds(2 * D, 128)] = jnp.zeros((ROWS, 128), BF)
    for head in range(HEADS):
        attend(head)
        if head % 4 == 3:
            project(*rest[head // 4])


def value_body(prob_ref, *refs):
    chunks = refs[:CHIPS]
    dv_ref, mine_ref, theirs_ref, grad_ref, acc_ref = refs[CHIPS:]
    for j in range(CHIPS):
        grad_ref[pl.ds(j * PAIR, PAIR), pl.ds(0, D)] = chunks[j][...]
    grad_ref[:, pl.ds(D, 128)] = jnp.zeros((ROWS, 128), BF)
    acc_ref[...] = jnp.zeros_like(acc_ref)

    def one(head):
        first, lanes = head_window(head)
        grad = keep(lanes, grad_ref[:, pl.ds(first, WIN)])
        acc_ref[:, pl.ds(first, WIN)] += jnp.dot(prob_ref[head], grad, preferred_element_type=F32)

    for head in range(HEADS):
        one(head)
    dv_ref[...] = acc_ref[:, pl.ds(0, D)].astype(BF)
    core = lax.axis_index("seq") % 2
    lead = D - HALF
    mine_ref[...] = dv_ref[:, pl.ds(pl.multiple_of(core * lead, 128), HALF)]
    theirs_ref[...] = dv_ref[:, pl.ds(pl.multiple_of((1 - core) * lead, 128), HALF)]


def weight_body(nt_ref, nt_other_ref, dv_ref, dv_other_ref, *out_refs):
    for tile in range(HALF // TILE):
        cols = pl.ds(tile * TILE, TILE)
        term = jnp.dot(nt_ref[...], dv_ref[:, cols], preferred_element_type=F32)
        term += jnp.dot(nt_other_ref[...], dv_other_ref[:, cols], preferred_element_type=F32)
        for j in range(4):
            out = out_refs[j]
            out[:, cols] = term[j * 4 * BLOCK : (j + 1) * 4 * BLOCK].astype(out.dtype)


def second_body(*refs):
    parts, gains, out_ref = refs[:4], refs[4:8], refs[8]
    gain = gains[0][...]
    for g in gains[1:]:
        gain = gain + g[...]
    gain = jnp.concatenate([gain, jnp.zeros((1, 2 * HALF - D), F32)], axis=1)
    rest = jnp.concatenate([gain[:, :HALF], gain[:, HALF:]], axis=0)
    total = parts[0][...]
    for part in parts[1:]:
        total = total + part[...].astype(F32)
    for i in range(16):
        rows = jnp.concatenate([total[i * 22 : i * 22 + 22], rest], axis=0)
        out_ref[i] = rows.astype(BF)


def third_body(parts_ref, mine_ref, theirs_ref):
    total = parts_ref[0].astype(F32)
    for i in range(1, 16):
        total = total + parts_ref[i].astype(F32)
    rest = jnp.concatenate([total[22:24], jnp.zeros((3, HALF), F32)], axis=0)
    low = jnp.concatenate([total[:11], rest], axis=0)
    high = jnp.concatenate([total[11:22], rest], axis=0)
    core = lax.axis_index("seq") % 2
    mine_ref[...] = jnp.where(core == 0, low, high)
    theirs_ref[...] = jnp.where(core == 0, high, low)


def last_body(factor):
    def body(mine_ref, other_ref, out_ref, gain_ref):
        core = lax.axis_index("seq") % 2
        mine, other = mine_ref[...] * factor, other_ref[...] * factor
        first = jnp.where(core == 0, mine, other)
        second = jnp.where(core == 0, other, mine)
        gain = (first + second)[11:13]
        out_ref[:, pl.ds(0, HALF)] = first[:11]
        out_ref[:, pl.ds(HALF, D - HALF)] = second[:11, 2 * HALF - D :]
        gain_ref[pl.ds(0, HALF)] = gain[0]
        gain_ref[pl.ds(HALF, D - HALF)] = gain[1, : D - HALF]

    return body


def input_body(*refs):
    xs, refs = refs[:CHIPS], refs[CHIPS:]
    qkv_ref, soft_ref, grad_ref, dv_ref, gain_ref, wbuf = refs[:6]
    outs, gain_out = refs[6 : 6 + CHIPS], refs[6 + CHIPS]
    dq_ref, dk_ref, g_ref, dn_ref = refs[7 + CHIPS :]
    tiles = [(0, 512), (512, 512), (1024, 384)]
    parts = [pl.ds(2 * D, D), pl.ds(0, 2 * D)]

    dq_ref[...] = jnp.zeros_like(dq_ref)
    dk_ref[...] = jnp.zeros_like(dk_ref)
    across = (((1,), (1,)), ((), ()))

    def one(head):
        first, lanes = head_window(head)
        query = keep(lanes, qkv_ref[:, pl.ds(first, WIN)])
        key = keep(lanes, qkv_ref[:, pl.ds(D + first, WIN)])
        value = keep(lanes, qkv_ref[:, pl.ds(2 * D + first, WIN)])
        grad = grad_ref[:, pl.ds(first, WIN)]
        d_probs = lax.dot_general(value, grad, across, preferred_element_type=F32)
        softmaxed = soft_ref[head]
        row_dot = jnp.sum(softmaxed * d_probs, axis=0, keepdims=True)
        d_scores = (softmaxed * (d_probs - row_dot) * SCALING).astype(BF)
        dk_ref[:, pl.ds(first, WIN)] += jnp.dot(d_scores, query, preferred_element_type=F32)
        dq_ref[:, pl.ds(first, WIN)] += lax.dot_general(
            d_scores, key, (((0,), (0,)), ((), ())), preferred_element_type=F32
        )

    for head in range(HEADS):
        one(head)
        if head % 4 == 3 and head < 15:
            rows = pl.ds(*tiles[head // 4])
            dn_ref[:, rows] = lax.dot_general(
                dv_ref[...], wbuf[rows, parts[0]], across, preferred_element_type=F32
            )
    g_ref[:, pl.ds(0, D)] = dq_ref[:, pl.ds(0, D)].astype(BF)
    g_ref[:, pl.ds(D, D)] = dk_ref[:, pl.ds(0, D)].astype(BF)
    for tile in tiles:
        rows = pl.ds(*tile)
        dn_ref[:, rows] += lax.dot_general(
            g_ref[...], wbuf[rows, parts[1]], across, preferred_element_type=F32
        )
    gain = gain_ref[...]
    gain_sum = jnp.zeros((1, D), F32)
    for k in range(SLOTS):
        rows = pl.ds(k % 2 * CHUNK, CHUNK)
        normalized, inv_std = normalize(xs[k // 2][rows, pl.ds(0, D)])
        d_normed = dn_ref[pl.ds(k * CHUNK, CHUNK), :]
        gain_sum = gain_sum + jnp.sum(d_normed * normalized, axis=0, keepdims=True)
        d_hat = d_normed * gain
        first_mean = jnp.mean(d_hat, axis=-1, keepdims=True)
        second_mean = jnp.mean(d_hat * normalized, axis=-1, keepdims=True)
        out = inv_std * (d_hat - first_mean - normalized * second_mean)
        outs[k // 2][rows, :] = out.astype(BF)
    gain_out[...] = gain_sum


def swap_seq(value, k):
    return lax.ppermute(value, "seq", [(i, i ^ k) for i in range(SLOTS)])


def swap_plane(value, j):
    pairs = []
    for dp in range(16):
        for seq in range(SLOTS):
            pairs.append((dp * SLOTS + seq, (dp ^ (4 * j if seq % 2 == 0 else j)) * SLOTS + seq))
    return lax.ppermute(value, ("dp", "seq"), pairs)


def exchange_plane(blocks):
    groups = []
    for core in range(2):
        for i in range(4):
            plane = [4 * i + j if core == 0 else 4 * j + i for j in range(4)]
            groups.append([dp * SLOTS + 2 * x + core for dp in plane for x in range(4)])
    return lax.all_to_all(
        blocks, ("dp", "seq"), split_axis=0, concat_axis=0, tiled=True, axis_index_groups=groups
    )


def swap_chips(chunks):
    return [chunks[0]] + [swap_seq(chunks[j], 2 * j) for j in range(1, CHIPS)]


def spread(rows, *clip, after=()):
    width = D + 128 * len(clip)
    mine, theirs = call(
        split_body,
        [shape((CHIPS, CHUNK, width), BF)] * 2,
        in_specs=[VMEM] + [SMEM] * len(clip),
        mib=8,
        data=10**6,
        name="split",
    )(rows, *clip)
    chunks = call(
        merge_body,
        [shape((PAIR, width), BF)] * CHIPS,
        in_specs=[VMEM, VMEM] + [pl.BlockSpec(memory_space=pl.ANY)] * len(after),
        mib=8,
        data=10**6,
        name="merge",
    )(mine, swap_seq(theirs, 1), *after)
    return swap_chips(chunks)


def gather(chunks):
    mine, theirs = call(
        part_body,
        [shape((CHIPS, CHUNK, D), BF)] * 2,
        mib=8,
        flops=2 * 10**10,
        data=10**6,
        name="part",
    )(*swap_chips(chunks))
    return call(join_body, shape((ROWS, D), BF), mib=8, data=10**6, name="join")(
        mine, swap_seq(theirs, 1)
    )


def four(rank, dims):
    return [shape(dims, F32)] + [shape(dims, BF)] * (rank - 1)


def shards(block_input, norm_gain, qkv_weight, frame_clip, out_grad):
    factor = 32768 ** (-0.5)
    gain = norm_gain.reshape(1, D)

    x = spread(block_input.reshape(ROWS, D), frame_clip)
    grads = spread(out_grad.reshape(ROWS, D), after=x[1:2])

    weight = call(
        load_body,
        shape((D, TRIPLE), BF),
        scratch=[pltpu.SemaphoreType.DMA(())],
        in_specs=[HBM],
        mib=2,
        data=24 * 10**6,
        name="load",
    )(qkv_weight)
    normed, clips = call(
        norm_body,
        [shape((ROWS, D), BF), shape((ROWS, 128), F32)],
        in_specs=[VMEM] * (CHIPS + 1) + [pl.BlockSpec(memory_space=pl.ANY)],
        mib=8,
        data=10**6,
        name="norm",
    )(*x, gain, weight)
    nt, nt_sent = call(
        turn_body,
        [shape((D, ROWS), BF)] * 2,
        scratch=[pltpu.VMEM((D, ROWS), F32)] * 2,
        mib=8,
        data=4 * 10**6,
        name="turn",
    )(normed)
    nt_other = swap_seq(nt_sent, 1)
    qkv, soft, probs = call(
        project_body,
        [
            shape((ROWS, PADDED), BF),
            shape((HEADS, ROWS, ROWS), F32),
            shape((HEADS, ROWS, ROWS), BF),
        ],
        scratch=[
            pltpu.VMEM((ROWS, ROWS), F32),
        ],
        mib=16,
        flops=5 * 10**9,
        data=40 * 10**6,
        name="project",
    )(clips, normed, weight)

    d_value, mine, theirs, grad_wide = call(
        value_body,
        [
            shape((ROWS, D), BF),
            shape((ROWS, HALF), BF),
            shape((ROWS, HALF), BF),
            shape((ROWS, WIDE), BF),
        ],
        scratch=[pltpu.VMEM((ROWS, WIDE), F32)],
        mib=16,
        flops=10**9,
        data=5 * 10**6,
        name="value",
    )(probs, *grads)
    other = swap_seq(theirs, 1)
    terms = call(
        weight_body,
        four(4, (4 * BLOCK, HALF)),
        mib=16,
        flops=11 * 10**8,
        data=6 * 10**6,
        name="weight",
    )(nt, nt_other, mine, other)
    terms = [terms[0]] + [swap_plane(terms[j], j) for j in range(1, 4)]

    results = call(
        input_body,
        [shape((PAIR, D), BF)] * CHIPS + [shape((1, D), F32)],
        scratch=[
            pltpu.VMEM((ROWS, WIDE), F32),
            pltpu.VMEM((ROWS, WIDE), F32),
            pltpu.VMEM((ROWS, 2 * D), BF),
            pltpu.VMEM((ROWS, D), F32),
        ],
        mib=16,
        flops=6 * 10**9,
        data=20 * 10**6,
        name="input",
    )(*x, qkv, soft, grad_wide, d_value, gain, weight)
    returned, gain_term = results[:CHIPS], results[CHIPS]
    gains = [gain_term] + [swap_plane(gain_term, j) for j in range(1, 4)]

    sums = call(second_body, shape((16, 24, HALF), BF), mib=16, data=5 * 10**6, name="second")(
        *terms, *gains
    )
    sums = exchange_plane(sums)
    mine, theirs = call(third_body, [shape((16, HALF), F32)] * 2, mib=8, data=10**6, name="third")(
        sums
    )
    weight_grad, gain_grad = call(
        last_body(factor),
        [shape((11, D), F32), shape((D,), F32)],
        mib=8,
        data=10**5,
        name="last",
    )(mine, swap_seq(theirs, 1))
    input_grad = gather(returned)
    return input_grad.reshape(block_input.shape), weight_grad, gain_grad


def solution(mesh):
    placed = (P("dp", "seq", None, None), P(), P(), P("dp", "seq"), P("dp", "seq", None, None))
    return jax.shard_map(
        shards,
        mesh=mesh,
        in_specs=placed,
        out_specs=(P("dp", "seq", None, None), P(("dp", "seq"), None), P()),
        check_vma=False,
    )
```

```python
import itertools

import jax
import jax.numpy as jnp
from jax import lax
from jax.experimental import pallas as pl
from jax.experimental.pallas import tpu as pltpu
from jax.sharding import PartitionSpec as P

HEADS = 16
HEAD_DIM = 88
D = 1408
TRIPLE = 3 * D
WIN = 256
PADDED = TRIPLE + 128
WIDE = D + 128
ROWS = 256
CHUNK = 32
SLOTS = 8
CHIPS = 4
PAIR = 2 * CHUNK
HALVES = 2
STEP = 16
SPAN = 128
TILE = 256
BLOCK = 88
HALF = 768
EPSILON = 1e-06
SCALING = HEAD_DIM ** (-0.5)
MASKED = -1e30

BF = jnp.bfloat16
F32 = jnp.float32


def shape(dims, dtype):
    return jax.ShapeDtypeStruct(dims, dtype)


def call(body, outs, scratch=(), in_specs=None, mib=16, flops=0, data=0, name=None):
    extra = {} if in_specs is None else {"in_specs": in_specs}
    return pl.pallas_call(
        body,
        out_shape=outs,
        scratch_shapes=list(scratch),
        compiler_params=pltpu.CompilerParams(vmem_limit_bytes=mib << 20),
        cost_estimate=pl.CostEstimate(flops=flops, bytes_accessed=data, transcendentals=0),
        name=name,
        **extra,
    )


VMEM = pl.BlockSpec(memory_space=pltpu.VMEM)
SMEM = pl.BlockSpec(memory_space=pltpu.SMEM)
HBM = pl.BlockSpec(memory_space=pl.ANY)


def head_window(head):
    first = (head * HEAD_DIM) // 128 * 128
    offset = head * HEAD_DIM - first
    lane = lax.broadcasted_iota(jnp.int32, (1, WIN), 1)
    return first, (lane >= offset) & (lane < offset + HEAD_DIM)


def keep(lanes, values):
    return jnp.where(lanes, values, jnp.zeros_like(values))


def normalize(rows):
    values = rows.astype(F32)
    centered = values - jnp.mean(values, axis=-1, keepdims=True)
    inv_std = lax.rsqrt(jnp.mean(centered * centered, axis=-1, keepdims=True) + EPSILON)
    return centered * inv_std, inv_std


def place():
    me = lax.axis_index("seq")
    return me // 2, me % 2


def part_rows(chip, core):
    return pl.ds(pl.multiple_of((2 * chip + core) * CHUNK, CHUNK), CHUNK)


def split_body(rows_ref, *refs):
    clip_ref, (mine_ref, theirs_ref) = refs[:-2], refs[-2:]
    chip, core = place()
    for j in range(CHIPS):
        mine_ref[j, :, pl.ds(0, D)] = rows_ref[part_rows(chip ^ j, core), :]
        theirs_ref[j, :, pl.ds(0, D)] = rows_ref[part_rows(chip ^ j, 1 - core), :]
    if clip_ref:
        clip = jnp.full((CHIPS, CHUNK, 128), clip_ref[0][0, 0], jnp.int32).astype(F32).astype(BF)
        mine_ref[:, :, pl.ds(D, 128)] = clip
        theirs_ref[:, :, pl.ds(D, 128)] = clip


def merge_body(mine_ref, other_ref, *refs):
    out_refs = refs[-CHIPS:]
    _, core = place()
    for j in range(CHIPS):
        out_refs[j][pl.ds(pl.multiple_of(core * CHUNK, CHUNK), CHUNK), :] = mine_ref[j]
        out_refs[j][pl.ds(pl.multiple_of((1 - core) * CHUNK, CHUNK), CHUNK), :] = other_ref[j]


def part_body(*refs):
    mine_ref, theirs_ref = refs[CHIPS:]
    _, core = place()
    for j in range(CHIPS):
        mine_ref[j] = refs[j][pl.ds(pl.multiple_of(core * CHUNK, CHUNK), CHUNK), :]
        theirs_ref[j] = refs[j][pl.ds(pl.multiple_of((1 - core) * CHUNK, CHUNK), CHUNK), :]


def join_body(mine_ref, other_ref, out_ref):
    chip, core = place()
    for j in range(CHIPS):
        out_ref[part_rows(chip ^ j, core), :] = mine_ref[j]
        out_ref[part_rows(chip ^ j, 1 - core), :] = other_ref[j]


def load_body(w_hbm, w_ref, sem):
    copy = pltpu.make_async_copy(w_hbm, w_ref, sem)
    copy.start()
    copy.wait()


def in_half(j, f, half):
    return pl.ds(half * SPAN + (2 * j + f) * STEP, STEP)


def norm_body(*refs):
    xs, (gain_ref, _, normed_ref, clip_ref) = refs[:CHIPS], refs[CHIPS:]
    for j in range(CHIPS):
        normalized, _ = normalize(xs[j][:, pl.ds(0, D)])
        normed = (normalized * gain_ref[...]).astype(BF)
        clip = xs[j][:, pl.ds(D, 128)].astype(F32)
        for f in range(2):
            for half in range(HALVES):
                first = f * CHUNK + half * STEP
                normed_ref[in_half(j, f, half), :] = normed[first : first + STEP]
            rows = pl.ds((2 * j + f) * STEP, STEP)
            clip_ref[rows, :] = clip[f * CHUNK : f * CHUNK + STEP]


def turn_body(normed_ref, mine_ref, theirs_ref, wide_ref, other_ref):
    core = lax.axis_index("seq") % 2
    for b in range(16):
        block = normed_ref[:, pl.ds(b * BLOCK // 128 * 128, 256 if b < 15 else 128)]
        offset = b * BLOCK % 128
        turned = jnp.transpose(block.astype(F32))[offset : offset + BLOCK]
        slot = lax.axis_index("dp") ^ b
        by_y = slot // 4 * 4 + b % 4
        by_z = slot % 4 * 4 + b // 4
        slot = jnp.where(core == 0, by_y, by_z)
        wide_ref[pl.ds(pl.multiple_of(slot * BLOCK, 8), BLOCK), :] = turned
        slot = jnp.where(core == 0, by_z, by_y)
        other_ref[pl.ds(pl.multiple_of(slot * BLOCK, 8), BLOCK), :] = turned
    mine_ref[...] = wide_ref[...].astype(BF)
    theirs_ref[...] = other_ref[...].astype(BF)


def project_body(clip_ref, normed_ref, wbuf, qkv_ref, soft_ref, prob_ref, bias_ref):
    first = [(0, 512), (512, 1152), (1664, 1152)]
    rest = [(2816, 384), (3200, 384), (3584, 384), (3968, 256)]

    def project(start, count):
        cols = pl.ds(start, count)
        out = jnp.dot(normed_ref[...], wbuf[:, cols], preferred_element_type=F32)
        qkv_ref[:, cols] = out.astype(BF)

    row = lax.broadcasted_iota(jnp.int32, (SPAN, SPAN), 0)
    col = lax.broadcasted_iota(jnp.int32, (SPAN, SPAN), 1)
    clip = clip_ref[...]
    kept = (clip == jnp.transpose(clip)) & (row % STEP == col % STEP)
    bias_ref[...] = jnp.where(kept, 0.0, MASKED).astype(F32)
    qkv_ref[:, pl.ds(TRIPLE, 128)] = jnp.zeros((ROWS, 128), BF)

    for start, count in first:
        project(start, count)

    def attend(head):
        start, lanes = head_window(head)
        for half in range(HALVES):
            rows = pl.ds(half * SPAN, SPAN)
            query = qkv_ref[rows, pl.ds(start, WIN)]
            key = keep(lanes, qkv_ref[rows, pl.ds(D + start, WIN)])
            scores = lax.dot_general(
                key, query, (((1,), (1,)), ((), ())), preferred_element_type=F32
            )
            scores = scores * SCALING + bias_ref[...]
            powers = jnp.exp(scores - jnp.max(scores, axis=0, keepdims=True))
            softmaxed = powers / jnp.sum(powers, axis=0, keepdims=True)
            soft_ref[head, half] = softmaxed
            prob_ref[head, half] = softmaxed.astype(BF)

    qkv_ref[:, pl.ds(2 * D, 128)] = jnp.zeros((ROWS, 128), BF)
    for head in range(HEADS):
        attend(head)
        if head % 4 == 3:
            project(*rest[head // 4])


def value_body(prob_ref, *refs):
    chunks = refs[:CHIPS]
    dv_ref, mine_ref, theirs_ref, grad_ref, acc_ref = refs[CHIPS:]
    for j in range(CHIPS):
        for f in range(2):
            for half in range(HALVES):
                rows = pl.ds(f * CHUNK + half * STEP, STEP)
                grad_ref[in_half(j, f, half), pl.ds(0, D)] = chunks[j][rows, :]
    grad_ref[:, pl.ds(D, 128)] = jnp.zeros((ROWS, 128), BF)
    acc_ref[...] = jnp.zeros_like(acc_ref)

    def one(head):
        first, lanes = head_window(head)
        for half in range(HALVES):
            at = pl.ds(half * SPAN, SPAN), pl.ds(first, WIN)
            grad = keep(lanes, grad_ref[at])
            acc_ref[at] += jnp.dot(prob_ref[head, half], grad, preferred_element_type=F32)

    for head in range(HEADS):
        one(head)
    dv_ref[...] = acc_ref[:, pl.ds(0, D)].astype(BF)
    core = lax.axis_index("seq") % 2
    lead = D - HALF
    mine_ref[...] = dv_ref[:, pl.ds(pl.multiple_of(core * lead, 128), HALF)]
    theirs_ref[...] = dv_ref[:, pl.ds(pl.multiple_of((1 - core) * lead, 128), HALF)]


def weight_body(nt_ref, nt_other_ref, dv_ref, dv_other_ref, *out_refs):
    for tile in range(HALF // TILE):
        cols = pl.ds(tile * TILE, TILE)
        term = jnp.dot(nt_ref[...], dv_ref[:, cols], preferred_element_type=F32)
        term += jnp.dot(nt_other_ref[...], dv_other_ref[:, cols], preferred_element_type=F32)
        for j in range(4):
            out = out_refs[j]
            out[:, cols] = term[j * 4 * BLOCK : (j + 1) * 4 * BLOCK].astype(out.dtype)


def second_body(*refs):
    parts, gains, out_ref = refs[:4], refs[4:6], refs[6]
    gain = gains[0][...]
    for g in gains[1:]:
        gain = gain + g[...]
    gain = jnp.concatenate([gain, jnp.zeros((1, 2 * HALF - D), F32)], axis=1)
    rest = jnp.concatenate([gain[:, :HALF], gain[:, HALF:]], axis=0)
    total = parts[0][...]
    for part in parts[1:]:
        total = total + part[...].astype(F32)
    for i in range(16):
        rows = jnp.concatenate([total[i * 22 : i * 22 + 22], rest], axis=0)
        out_ref[i] = rows.astype(BF)


def third_body(parts_ref, mine_ref, theirs_ref):
    total = parts_ref[0].astype(F32)
    for i in range(1, 16):
        total = total + parts_ref[i].astype(F32)
    rest = jnp.concatenate([total[22:24], jnp.zeros((3, HALF), F32)], axis=0)
    low = jnp.concatenate([total[:11], rest], axis=0)
    high = jnp.concatenate([total[11:22], rest], axis=0)
    core = lax.axis_index("seq") % 2
    mine_ref[...] = jnp.where(core == 0, low, high)
    theirs_ref[...] = jnp.where(core == 0, high, low)


def last_body(factor):
    def body(mine_ref, other_ref, out_ref, gain_ref):
        core = lax.axis_index("seq") % 2
        mine, other = mine_ref[...] * factor, other_ref[...] * factor
        first = jnp.where(core == 0, mine, other)
        second = jnp.where(core == 0, other, mine)
        gain = (first + second)[11:13]
        out_ref[:, pl.ds(0, HALF)] = first[:11]
        out_ref[:, pl.ds(HALF, D - HALF)] = second[:11, 2 * HALF - D :]
        gain_ref[pl.ds(0, HALF)] = gain[0]
        gain_ref[pl.ds(HALF, D - HALF)] = gain[1, : D - HALF]

    return body


def input_body(*refs):
    xs, refs = refs[:CHIPS], refs[CHIPS:]
    qkv_ref, soft_ref, grad_ref, dv_ref, gain_ref, wbuf = refs[:6]
    outs, gain_out = refs[6 : 6 + CHIPS], refs[6 + CHIPS]
    dq_ref, dk_ref, g_ref, dn_ref = refs[7 + CHIPS :]
    tiles = [(0, 512), (512, 512), (1024, 384)]
    sides = [pl.ds(2 * D, D), pl.ds(0, 2 * D)]

    dq_ref[...] = jnp.zeros_like(dq_ref)
    dk_ref[...] = jnp.zeros_like(dk_ref)
    across = (((1,), (1,)), ((), ()))

    def one(head):
        first, lanes = head_window(head)
        lane = pl.ds(first, WIN)
        query = keep(lanes, qkv_ref[:, lane])
        key = keep(lanes, qkv_ref[:, pl.ds(D + first, WIN)])
        value = keep(lanes, qkv_ref[:, pl.ds(2 * D + first, WIN)])
        parts = []
        for half in range(HALVES):
            d_probs = lax.dot_general(
                value[half * SPAN : (half + 1) * SPAN],
                grad_ref[pl.ds(half * SPAN, SPAN), lane],
                across,
                preferred_element_type=F32,
            )
            softmaxed = soft_ref[head, half]
            row_dot = jnp.sum(softmaxed * d_probs, axis=0, keepdims=True)
            parts.append((softmaxed * (d_probs - row_dot) * SCALING).astype(BF))
        none = jnp.zeros((SPAN, SPAN), BF)
        d_scores = jnp.concatenate(
            [jnp.concatenate([parts[0], none], 1), jnp.concatenate([none, parts[1]], 1)], 0
        )
        dk_ref[:, lane] += jnp.dot(d_scores, query, preferred_element_type=F32)
        dq_ref[:, lane] += lax.dot_general(
            d_scores, key, (((0,), (0,)), ((), ())), preferred_element_type=F32
        )

    for head in range(HEADS):
        one(head)
        if head % 4 == 3 and head < 15:
            rows = pl.ds(*tiles[head // 4])
            dn_ref[:, rows] = lax.dot_general(
                dv_ref[...], wbuf[rows, sides[0]], across, preferred_element_type=F32
            )
    g_ref[:, pl.ds(0, D)] = dq_ref[:, pl.ds(0, D)].astype(BF)
    g_ref[:, pl.ds(D, D)] = dk_ref[:, pl.ds(0, D)].astype(BF)
    for tile in tiles:
        rows = pl.ds(*tile)
        dn_ref[:, rows] += lax.dot_general(
            g_ref[...], wbuf[rows, sides[1]], across, preferred_element_type=F32
        )
    gain = gain_ref[...]
    gain_sum = jnp.zeros((1, D), F32)
    for j, f, half in itertools.product(range(CHIPS), range(2), range(HALVES)):
        rows = pl.ds(f * CHUNK + half * STEP, STEP)
        normalized, inv_std = normalize(xs[j][rows, pl.ds(0, D)])
        d_normed = dn_ref[in_half(j, f, half), :]
        gain_sum = gain_sum + jnp.sum(d_normed * normalized, axis=0, keepdims=True)
        d_hat = d_normed * gain
        first_mean = jnp.mean(d_hat, axis=-1, keepdims=True)
        second_mean = jnp.mean(d_hat * normalized, axis=-1, keepdims=True)
        out = inv_std * (d_hat - first_mean - normalized * second_mean)
        outs[j][rows, :] = out.astype(BF)
    gain_out[...] = gain_sum


def swap_seq(value, k):
    return lax.ppermute(value, "seq", [(i, i ^ k) for i in range(SLOTS)])


def swap_plane(value, j):
    pairs = []
    for dp in range(16):
        for seq in range(SLOTS):
            pairs.append((dp * SLOTS + seq, (dp ^ (4 * j if seq % 2 == 0 else j)) * SLOTS + seq))
    return lax.ppermute(value, ("dp", "seq"), pairs)


def exchange_plane(blocks):
    groups = []
    for core in range(2):
        for i in range(4):
            plane = [4 * i + j if core == 0 else 4 * j + i for j in range(4)]
            groups.append([dp * SLOTS + 2 * x + core for dp in plane for x in range(4)])
    return lax.all_to_all(
        blocks, ("dp", "seq"), split_axis=0, concat_axis=0, tiled=True, axis_index_groups=groups
    )


def swap_chips(chunks):
    moved = {j: swap_seq(chunks[j], 2 * j) for j in (1, 3, 2)}
    return [chunks[0]] + [moved[j] for j in range(1, CHIPS)]


def spread(rows, *clip, after=()):
    width = D + 128 * len(clip)
    mine, theirs = call(
        split_body,
        [shape((CHIPS, CHUNK, width), BF)] * 2,
        in_specs=[VMEM] + [SMEM] * len(clip),
        mib=8,
        data=10**6,
        name="split",
    )(rows, *clip)
    chunks = call(
        merge_body,
        [shape((PAIR, width), BF)] * CHIPS,
        in_specs=[VMEM, VMEM] + [pl.BlockSpec(memory_space=pl.ANY)] * len(after),
        mib=8,
        data=10**6,
        name="merge",
    )(mine, swap_seq(theirs, 1), *after)
    return swap_chips(chunks)


def gather(chunks):
    mine, theirs = call(
        part_body,
        [shape((CHIPS, CHUNK, D), BF)] * 2,
        mib=8,
        flops=2 * 10**10,
        data=10**6,
        name="part",
    )(*swap_chips(chunks))
    return call(join_body, shape((ROWS, D), BF), mib=8, data=10**6, name="join")(
        mine, swap_seq(theirs, 1)
    )


def four(rank, dims):
    return [shape(dims, F32)] + [shape(dims, BF)] * (rank - 1)


def shards(block_input, norm_gain, qkv_weight, frame_clip, out_grad):
    factor = 32768 ** (-0.5)
    gain = norm_gain.reshape(1, D)

    x = spread(block_input.reshape(ROWS, D), frame_clip)
    grads = spread(out_grad.reshape(ROWS, D), after=x[1:2])

    weight = call(
        load_body,
        shape((D, TRIPLE), BF),
        scratch=[pltpu.SemaphoreType.DMA(())],
        in_specs=[HBM],
        mib=2,
        data=24 * 10**6,
        name="load",
    )(qkv_weight)
    normed, clips = call(
        norm_body,
        [shape((ROWS, D), BF), shape((SPAN, 128), F32)],
        in_specs=[VMEM] * (CHIPS + 1) + [pl.BlockSpec(memory_space=pl.ANY)],
        mib=8,
        data=10**6,
        name="norm",
    )(*x, gain, weight)
    nt, nt_sent = call(
        turn_body,
        [shape((D, ROWS), BF)] * 2,
        scratch=[pltpu.VMEM((D, ROWS), F32)] * 2,
        mib=8,
        data=4 * 10**6,
        name="turn",
    )(normed)
    nt_other = swap_seq(nt_sent, 1)
    qkv, soft, probs = call(
        project_body,
        [
            shape((ROWS, PADDED), BF),
            shape((HEADS, HALVES, SPAN, SPAN), F32),
            shape((HEADS, HALVES, SPAN, SPAN), BF),
        ],
        scratch=[
            pltpu.VMEM((SPAN, SPAN), F32),
        ],
        mib=16,
        flops=5 * 10**9,
        data=40 * 10**6,
        name="project",
    )(clips, normed, weight)

    d_value, mine, theirs, grad_wide = call(
        value_body,
        [
            shape((ROWS, D), BF),
            shape((ROWS, HALF), BF),
            shape((ROWS, HALF), BF),
            shape((ROWS, WIDE), BF),
        ],
        scratch=[pltpu.VMEM((ROWS, WIDE), F32)],
        mib=16,
        flops=10**9,
        data=5 * 10**6,
        name="value",
    )(probs, *grads)
    other = swap_seq(theirs, 1)
    terms = call(
        weight_body,
        four(4, (4 * BLOCK, HALF)),
        mib=16,
        flops=11 * 10**8,
        data=6 * 10**6,
        name="weight",
    )(nt, nt_other, mine, other)
    terms = [terms[0]] + [swap_plane(terms[j], j) for j in range(1, 4)]

    results = call(
        input_body,
        [shape((PAIR, D), BF)] * CHIPS + [shape((1, D), F32)],
        scratch=[
            pltpu.VMEM((ROWS, WIDE), F32),
            pltpu.VMEM((ROWS, WIDE), F32),
            pltpu.VMEM((ROWS, 2 * D), BF),
            pltpu.VMEM((ROWS, D), F32),
        ],
        mib=16,
        flops=6 * 10**9,
        data=20 * 10**6,
        name="input",
    )(*x, qkv, soft, grad_wide, d_value, gain, weight)
    returned, gain_term = results[:CHIPS], results[CHIPS]
    gain_term = gain_term + swap_plane(gain_term, 1)
    gains = [gain_term, swap_plane(gain_term, 3)]

    sums = call(second_body, shape((16, 24, HALF), BF), mib=16, data=5 * 10**6, name="second")(
        *terms, *gains
    )
    sums = exchange_plane(sums)
    mine, theirs = call(third_body, [shape((16, HALF), F32)] * 2, mib=8, data=10**6, name="third")(
        sums
    )
    weight_grad, gain_grad = call(
        last_body(factor),
        [shape((11, D), F32), shape((D,), F32)],
        mib=8,
        data=10**5,
        name="last",
    )(mine, swap_seq(theirs, 1))
    input_grad = gather(returned)
    return input_grad.reshape(block_input.shape), weight_grad, gain_grad


def solution(mesh):
    placed = (P("dp", "seq", None, None), P(), P(), P("dp", "seq"), P("dp", "seq", None, None))
    return jax.shard_map(
        shards,
        mesh=mesh,
        in_specs=placed,
        out_specs=(P("dp", "seq", None, None), P(("dp", "seq"), None), P()),
        check_vma=False,
    )
```

```python
import itertools

import jax
import jax.numpy as jnp
from jax import lax
from jax.experimental import pallas as pl
from jax.experimental.pallas import tpu as pltpu
from jax.sharding import PartitionSpec as P

HEADS = 16
HEAD_DIM = 88
D = 1408
TRIPLE = 3 * D
WIN = 256
PADDED = TRIPLE + 128
WIDE = D + 128
ROWS = 256
CHUNK = 32
SLOTS = 8
CHIPS = 4
PAIR = 2 * CHUNK
HALVES = 2
STEP = 16
SPAN = 128
TILE = 256
BLOCK = 88
HALF = 768
EPSILON = 1e-06
SCALING = HEAD_DIM ** (-0.5)
MASKED = -1e30

BF = jnp.bfloat16
F32 = jnp.float32


def shape(dims, dtype):
    return jax.ShapeDtypeStruct(dims, dtype)


def call(body, outs, scratch=(), in_specs=None, mib=16, flops=0, data=0, name=None):
    extra = {} if in_specs is None else {"in_specs": in_specs}
    return pl.pallas_call(
        body,
        out_shape=outs,
        scratch_shapes=list(scratch),
        compiler_params=pltpu.CompilerParams(vmem_limit_bytes=mib << 20),
        cost_estimate=pl.CostEstimate(flops=flops, bytes_accessed=data, transcendentals=0),
        name=name,
        **extra,
    )


VMEM = pl.BlockSpec(memory_space=pltpu.VMEM)
SMEM = pl.BlockSpec(memory_space=pltpu.SMEM)
HBM = pl.BlockSpec(memory_space=pl.ANY)


def head_window(head):
    first = (head * HEAD_DIM) // 128 * 128
    offset = head * HEAD_DIM - first
    lane = lax.broadcasted_iota(jnp.int32, (1, WIN), 1)
    return first, (lane >= offset) & (lane < offset + HEAD_DIM)


def keep(lanes, values):
    return jnp.where(lanes, values, jnp.zeros_like(values))


def normalize(rows):
    values = rows.astype(F32)
    centered = values - jnp.mean(values, axis=-1, keepdims=True)
    inv_std = lax.rsqrt(jnp.mean(centered * centered, axis=-1, keepdims=True) + EPSILON)
    return centered * inv_std, inv_std


def place():
    me = lax.axis_index("seq")
    return me // 2, me % 2


def part_rows(chip, core):
    return pl.ds(pl.multiple_of((2 * chip + core) * CHUNK, CHUNK), CHUNK)


def split_body(rows_ref, *refs):
    clip_ref, (mine_ref, theirs_ref) = refs[:-2], refs[-2:]
    chip, core = place()
    for j in range(CHIPS):
        mine_ref[j, :, pl.ds(0, D)] = rows_ref[part_rows(chip ^ j, core), :]
        theirs_ref[j, :, pl.ds(0, D)] = rows_ref[part_rows(chip ^ j, 1 - core), :]
    if clip_ref:
        clip = jnp.full((CHIPS, CHUNK, 128), clip_ref[0][0, 0], jnp.int32).astype(F32).astype(BF)
        mine_ref[:, :, pl.ds(D, 128)] = clip
        theirs_ref[:, :, pl.ds(D, 128)] = clip


def merge_body(mine_ref, other_ref, *refs):
    out_refs = refs[-CHIPS:]
    _, core = place()
    for j in range(CHIPS):
        out_refs[j][pl.ds(pl.multiple_of(core * CHUNK, CHUNK), CHUNK), :] = mine_ref[j]
        out_refs[j][pl.ds(pl.multiple_of((1 - core) * CHUNK, CHUNK), CHUNK), :] = other_ref[j]


def part_body(*refs):
    mine_ref, theirs_ref = refs[CHIPS:]
    _, core = place()
    for j in range(CHIPS):
        mine_ref[j] = refs[j][pl.ds(pl.multiple_of(core * CHUNK, CHUNK), CHUNK), :]
        theirs_ref[j] = refs[j][pl.ds(pl.multiple_of((1 - core) * CHUNK, CHUNK), CHUNK), :]


def join_body(mine_ref, other_ref, out_ref):
    chip, core = place()
    for j in range(CHIPS):
        out_ref[part_rows(chip ^ j, core), :] = mine_ref[j]
        out_ref[part_rows(chip ^ j, 1 - core), :] = other_ref[j]


def load_body(w_hbm, w_ref, sem):
    copy = pltpu.make_async_copy(w_hbm, w_ref, sem)
    copy.start()
    copy.wait()


def in_half(j, f, half):
    return pl.ds(half * SPAN + (2 * j + f) * STEP, STEP)


def norm_body(*refs):
    xs, (gain_ref, _, normed_ref, clip_ref) = refs[:CHIPS], refs[CHIPS:]
    for j in range(CHIPS):
        normalized, _ = normalize(xs[j][:, pl.ds(0, D)])
        normed = (normalized * gain_ref[...]).astype(BF)
        clip = xs[j][:, pl.ds(D, 128)].astype(F32)
        for f in range(2):
            for half in range(HALVES):
                first = f * CHUNK + half * STEP
                normed_ref[in_half(j, f, half), :] = normed[first : first + STEP]
            rows = pl.ds((2 * j + f) * STEP, STEP)
            clip_ref[rows, :] = clip[f * CHUNK : f * CHUNK + STEP]


def turn_body(normed_ref, mine_ref, theirs_ref, wide_ref, other_ref):
    core = lax.axis_index("seq") % 2
    for b in range(16):
        block = normed_ref[:, pl.ds(b * BLOCK // 128 * 128, 256 if b < 15 else 128)]
        offset = b * BLOCK % 128
        turned = jnp.transpose(block.astype(F32))[offset : offset + BLOCK]
        slot = lax.axis_index("dp") ^ b
        by_y = slot // 4 * 4 + b % 4
        by_z = slot % 4 * 4 + b // 4
        slot = jnp.where(core == 0, by_y, by_z)
        wide_ref[pl.ds(pl.multiple_of(slot * BLOCK, 8), BLOCK), :] = turned
        slot = jnp.where(core == 0, by_z, by_y)
        other_ref[pl.ds(pl.multiple_of(slot * BLOCK, 8), BLOCK), :] = turned
    mine_ref[...] = wide_ref[...].astype(BF)
    theirs_ref[...] = other_ref[...].astype(BF)


def project_body(clip_ref, normed_ref, wbuf, qkv_ref, soft_ref, prob_ref, bias_ref):
    first = [(0, 512), (512, 1152), (1664, 1152)]
    rest = [(2816, 384), (3200, 384), (3584, 384), (3968, 256)]

    def project(start, count):
        cols = pl.ds(start, count)
        out = jnp.dot(normed_ref[...], wbuf[:, cols], preferred_element_type=F32)
        qkv_ref[:, cols] = out.astype(BF)

    row = lax.broadcasted_iota(jnp.int32, (SPAN, SPAN), 0)
    col = lax.broadcasted_iota(jnp.int32, (SPAN, SPAN), 1)
    clip = clip_ref[...]
    kept = (clip == jnp.transpose(clip)) & (row % STEP == col % STEP)
    bias_ref[...] = jnp.where(kept, 0.0, MASKED).astype(F32)
    qkv_ref[:, pl.ds(TRIPLE, 128)] = jnp.zeros((ROWS, 128), BF)

    for start, count in first:
        project(start, count)

    def attend(head):
        start, lanes = head_window(head)
        for half in range(HALVES):
            rows = pl.ds(half * SPAN, SPAN)
            query = qkv_ref[rows, pl.ds(start, WIN)]
            key = keep(lanes, qkv_ref[rows, pl.ds(D + start, WIN)])
            scores = lax.dot_general(
                key, query, (((1,), (1,)), ((), ())), preferred_element_type=F32
            )
            scores = scores * SCALING + bias_ref[...]
            powers = jnp.exp(scores - jnp.max(scores, axis=0, keepdims=True))
            softmaxed = powers / jnp.sum(powers, axis=0, keepdims=True)
            soft_ref[head, half] = softmaxed
            prob_ref[head, half] = softmaxed.astype(BF)

    qkv_ref[:, pl.ds(2 * D, 128)] = jnp.zeros((ROWS, 128), BF)
    for head in range(HEADS):
        attend(head)
        if head % 4 == 3:
            project(*rest[head // 4])


def value_body(prob_ref, *refs):
    chunks = refs[:CHIPS]
    dv_ref, mine_ref, theirs_ref, grad_ref, acc_ref = refs[CHIPS:]
    for j in range(CHIPS):
        for f in range(2):
            for half in range(HALVES):
                rows = pl.ds(f * CHUNK + half * STEP, STEP)
                grad_ref[in_half(j, f, half), pl.ds(0, D)] = chunks[j][rows, :]
    grad_ref[:, pl.ds(D, 128)] = jnp.zeros((ROWS, 128), BF)
    acc_ref[...] = jnp.zeros_like(acc_ref)

    def one(head):
        first, lanes = head_window(head)
        for half in range(HALVES):
            at = pl.ds(half * SPAN, SPAN), pl.ds(first, WIN)
            grad = keep(lanes, grad_ref[at])
            acc_ref[at] += jnp.dot(prob_ref[head, half], grad, preferred_element_type=F32)

    for head in range(HEADS):
        one(head)
    dv_ref[...] = acc_ref[:, pl.ds(0, D)].astype(BF)
    core = lax.axis_index("seq") % 2
    lead = D - HALF
    mine_ref[...] = dv_ref[:, pl.ds(pl.multiple_of(core * lead, 128), HALF)]
    theirs_ref[...] = dv_ref[:, pl.ds(pl.multiple_of((1 - core) * lead, 128), HALF)]


def own_body(nt_ref, dv_ref, out_ref):
    for tile in range(HALF // TILE):
        cols = pl.ds(tile * TILE, TILE)
        out_ref[:, cols] = jnp.dot(nt_ref[...], dv_ref[:, cols], preferred_element_type=F32)


def weight_body(own_ref, nt_other_ref, dv_other_ref, *out_refs):
    for tile in range(HALF // TILE):
        cols = pl.ds(tile * TILE, TILE)
        term = jnp.dot(nt_other_ref[...], dv_other_ref[:, cols], preferred_element_type=F32)
        term += own_ref[:, cols]
        for j in range(4):
            out = out_refs[j]
            out[:, cols] = term[j * 4 * BLOCK : (j + 1) * 4 * BLOCK].astype(out.dtype)


def second_body(*refs):
    parts, gains, out_ref = refs[:4], refs[4:6], refs[6]
    gain = gains[0][...]
    for g in gains[1:]:
        gain = gain + g[...]
    gain = jnp.concatenate([gain, jnp.zeros((1, 2 * HALF - D), F32)], axis=1)
    rest = jnp.concatenate([gain[:, :HALF], gain[:, HALF:]], axis=0)
    total = parts[0][...]
    for part in parts[1:]:
        total = total + part[...].astype(F32)
    for i in range(16):
        rows = jnp.concatenate([total[i * 22 : i * 22 + 22], rest], axis=0)
        out_ref[i] = rows.astype(BF)


def third_body(parts_ref, mine_ref, theirs_ref):
    total = parts_ref[0].astype(F32)
    for i in range(1, 16):
        total = total + parts_ref[i].astype(F32)
    rest = jnp.concatenate([total[22:24], jnp.zeros((3, HALF), F32)], axis=0)
    low = jnp.concatenate([total[:11], rest], axis=0)
    high = jnp.concatenate([total[11:22], rest], axis=0)
    core = lax.axis_index("seq") % 2
    mine_ref[...] = jnp.where(core == 0, low, high)
    theirs_ref[...] = jnp.where(core == 0, high, low)


def last_body(factor):
    def body(mine_ref, other_ref, out_ref, gain_ref):
        core = lax.axis_index("seq") % 2
        mine, other = mine_ref[...] * factor, other_ref[...] * factor
        first = jnp.where(core == 0, mine, other)
        second = jnp.where(core == 0, other, mine)
        gain = (first + second)[11:13]
        out_ref[:, pl.ds(0, HALF)] = first[:11]
        out_ref[:, pl.ds(HALF, D - HALF)] = second[:11, 2 * HALF - D :]
        gain_ref[pl.ds(0, HALF)] = gain[0]
        gain_ref[pl.ds(HALF, D - HALF)] = gain[1, : D - HALF]

    return body


def input_body(*refs):
    xs, refs = refs[:CHIPS], refs[CHIPS:]
    qkv_ref, soft_ref, grad_ref, dv_ref, gain_ref, wbuf = refs[:6]
    outs, gain_out = refs[6 : 6 + CHIPS], refs[6 + CHIPS]
    dq_ref, dk_ref, g_ref, dn_ref = refs[7 + CHIPS :]
    tiles = [(0, 512), (512, 512), (1024, 384)]
    sides = [pl.ds(2 * D, D), pl.ds(0, 2 * D)]

    dq_ref[...] = jnp.zeros_like(dq_ref)
    dk_ref[...] = jnp.zeros_like(dk_ref)
    across = (((1,), (1,)), ((), ()))

    def one(head):
        first, lanes = head_window(head)
        lane = pl.ds(first, WIN)
        query = keep(lanes, qkv_ref[:, lane])
        key = keep(lanes, qkv_ref[:, pl.ds(D + first, WIN)])
        value = keep(lanes, qkv_ref[:, pl.ds(2 * D + first, WIN)])
        parts = []
        for half in range(HALVES):
            d_probs = lax.dot_general(
                value[half * SPAN : (half + 1) * SPAN],
                grad_ref[pl.ds(half * SPAN, SPAN), lane],
                across,
                preferred_element_type=F32,
            )
            softmaxed = soft_ref[head, half]
            row_dot = jnp.sum(softmaxed * d_probs, axis=0, keepdims=True)
            parts.append((softmaxed * (d_probs - row_dot) * SCALING).astype(BF))
        none = jnp.zeros((SPAN, SPAN), BF)
        d_scores = jnp.concatenate(
            [jnp.concatenate([parts[0], none], 1), jnp.concatenate([none, parts[1]], 1)], 0
        )
        dk_ref[:, lane] += jnp.dot(d_scores, query, preferred_element_type=F32)
        dq_ref[:, lane] += lax.dot_general(
            d_scores, key, (((0,), (0,)), ((), ())), preferred_element_type=F32
        )

    for head in range(HEADS):
        one(head)
        if head % 4 == 3 and head < 15:
            rows = pl.ds(*tiles[head // 4])
            dn_ref[:, rows] = lax.dot_general(
                dv_ref[...], wbuf[rows, sides[0]], across, preferred_element_type=F32
            )
    g_ref[:, pl.ds(0, D)] = dq_ref[:, pl.ds(0, D)].astype(BF)
    g_ref[:, pl.ds(D, D)] = dk_ref[:, pl.ds(0, D)].astype(BF)
    for tile in tiles:
        rows = pl.ds(*tile)
        dn_ref[:, rows] += lax.dot_general(
            g_ref[...], wbuf[rows, sides[1]], across, preferred_element_type=F32
        )
    gain = gain_ref[...]
    gain_sum = jnp.zeros((1, D), F32)
    for j, f, half in itertools.product(range(CHIPS), range(2), range(HALVES)):
        rows = pl.ds(f * CHUNK + half * STEP, STEP)
        normalized, inv_std = normalize(xs[j][rows, pl.ds(0, D)])
        d_normed = dn_ref[in_half(j, f, half), :]
        gain_sum = gain_sum + jnp.sum(d_normed * normalized, axis=0, keepdims=True)
        d_hat = d_normed * gain
        first_mean = jnp.mean(d_hat, axis=-1, keepdims=True)
        second_mean = jnp.mean(d_hat * normalized, axis=-1, keepdims=True)
        out = inv_std * (d_hat - first_mean - normalized * second_mean)
        outs[j][rows, :] = out.astype(BF)
    gain_out[...] = gain_sum


def swap_seq(value, k):
    return lax.ppermute(value, "seq", [(i, i ^ k) for i in range(SLOTS)])


def swap_plane(value, j):
    pairs = []
    for dp in range(16):
        for seq in range(SLOTS):
            pairs.append((dp * SLOTS + seq, (dp ^ (4 * j if seq % 2 == 0 else j)) * SLOTS + seq))
    return lax.ppermute(value, ("dp", "seq"), pairs)


def exchange_plane(blocks):
    groups = []
    for core in range(2):
        for i in range(4):
            plane = [4 * i + j if core == 0 else 4 * j + i for j in range(4)]
            groups.append([dp * SLOTS + 2 * x + core for dp in plane for x in range(4)])
    return lax.all_to_all(
        blocks, ("dp", "seq"), split_axis=0, concat_axis=0, tiled=True, axis_index_groups=groups
    )


def swap_chips(chunks):
    moved = {j: swap_seq(chunks[j], 2 * j) for j in (1, 3, 2)}
    return [chunks[0]] + [moved[j] for j in range(1, CHIPS)]


def spread(rows, *clip, after=()):
    width = D + 128 * len(clip)
    mine, theirs = call(
        split_body,
        [shape((CHIPS, CHUNK, width), BF)] * 2,
        in_specs=[VMEM] + [SMEM] * len(clip),
        mib=8,
        data=10**6,
        name="split",
    )(rows, *clip)
    chunks = call(
        merge_body,
        [shape((PAIR, width), BF)] * CHIPS,
        in_specs=[VMEM, VMEM] + [pl.BlockSpec(memory_space=pl.ANY)] * len(after),
        mib=8,
        data=10**6,
        name="merge",
    )(mine, swap_seq(theirs, 1), *after)
    return swap_chips(chunks)


def gather(chunks):
    mine, theirs = call(
        part_body,
        [shape((CHIPS, CHUNK, D), BF)] * 2,
        mib=8,
        flops=2 * 10**10,
        data=10**6,
        name="part",
    )(*swap_chips(chunks))
    return call(join_body, shape((ROWS, D), BF), mib=8, data=10**6, name="join")(
        mine, swap_seq(theirs, 1)
    )


def four(rank, dims):
    return [shape(dims, F32)] + [shape(dims, BF)] * (rank - 1)


def shards(block_input, norm_gain, qkv_weight, frame_clip, out_grad):
    factor = 32768 ** (-0.5)
    gain = norm_gain.reshape(1, D)

    x = spread(block_input.reshape(ROWS, D), frame_clip)
    grads = spread(out_grad.reshape(ROWS, D), after=x[1:2])

    weight = call(
        load_body,
        shape((D, TRIPLE), BF),
        scratch=[pltpu.SemaphoreType.DMA(())],
        in_specs=[HBM],
        mib=2,
        data=24 * 10**6,
        name="load",
    )(qkv_weight)
    normed, clips = call(
        norm_body,
        [shape((ROWS, D), BF), shape((SPAN, 128), F32)],
        in_specs=[VMEM] * (CHIPS + 1) + [pl.BlockSpec(memory_space=pl.ANY)],
        mib=8,
        data=10**6,
        name="norm",
    )(*x, gain, weight)
    nt, nt_sent = call(
        turn_body,
        [shape((D, ROWS), BF)] * 2,
        scratch=[pltpu.VMEM((D, ROWS), F32)] * 2,
        mib=8,
        data=4 * 10**6,
        name="turn",
    )(normed)
    nt_other = swap_seq(nt_sent, 1)
    qkv, soft, probs = call(
        project_body,
        [
            shape((ROWS, PADDED), BF),
            shape((HEADS, HALVES, SPAN, SPAN), F32),
            shape((HEADS, HALVES, SPAN, SPAN), BF),
        ],
        scratch=[
            pltpu.VMEM((SPAN, SPAN), F32),
        ],
        mib=16,
        flops=5 * 10**9,
        data=40 * 10**6,
        name="project",
    )(clips, normed, weight)

    d_value, mine, theirs, grad_wide = call(
        value_body,
        [
            shape((ROWS, D), BF),
            shape((ROWS, HALF), BF),
            shape((ROWS, HALF), BF),
            shape((ROWS, WIDE), BF),
        ],
        scratch=[pltpu.VMEM((ROWS, WIDE), F32)],
        mib=16,
        flops=10**9,
        data=5 * 10**6,
        name="value",
    )(probs, *grads)
    other = swap_seq(theirs, 1)
    own = call(
        own_body, shape((D, HALF), F32), mib=16, flops=5 * 10**8, data=6 * 10**6, name="own"
    )(nt, mine)
    terms = call(
        weight_body,
        four(4, (4 * BLOCK, HALF)),
        mib=16,
        flops=11 * 10**8,
        data=6 * 10**6,
        name="weight",
    )(own, nt_other, other)
    terms = [terms[0]] + [swap_plane(terms[j], j) for j in range(1, 4)]

    results = call(
        input_body,
        [shape((PAIR, D), BF)] * CHIPS + [shape((1, D), F32)],
        scratch=[
            pltpu.VMEM((ROWS, WIDE), F32),
            pltpu.VMEM((ROWS, WIDE), F32),
            pltpu.VMEM((ROWS, 2 * D), BF),
            pltpu.VMEM((ROWS, D), F32),
        ],
        mib=16,
        flops=6 * 10**9,
        data=20 * 10**6,
        name="input",
    )(*x, qkv, soft, grad_wide, d_value, gain, weight)
    returned, gain_term = results[:CHIPS], results[CHIPS]
    gain_term = gain_term + swap_plane(gain_term, 1)
    gains = [gain_term, swap_plane(gain_term, 3)]

    sums = call(second_body, shape((16, 24, HALF), BF), mib=16, data=5 * 10**6, name="second")(
        *terms, *gains
    )
    sums = exchange_plane(sums)
    mine, theirs = call(third_body, [shape((16, HALF), F32)] * 2, mib=8, data=10**6, name="third")(
        sums
    )
    weight_grad, gain_grad = call(
        last_body(factor),
        [shape((11, D), F32), shape((D,), F32)],
        mib=8,
        data=10**5,
        name="last",
    )(mine, swap_seq(theirs, 1))
    input_grad = gather(returned)
    return input_grad.reshape(block_input.shape), weight_grad, gain_grad


def solution(mesh):
    placed = (P("dp", "seq", None, None), P(), P(), P("dp", "seq"), P("dp", "seq", None, None))
    return jax.shard_map(
        shards,
        mesh=mesh,
        in_specs=placed,
        out_specs=(P("dp", "seq", None, None), P(("dp", "seq"), None), P()),
        check_vma=False,
    )
```

```python
import itertools

import jax
import jax.numpy as jnp
from jax import lax
from jax.experimental import pallas as pl
from jax.experimental.pallas import tpu as pltpu
from jax.sharding import PartitionSpec as P

HEADS = 16
HEAD_DIM = 88
D = 1408
TRIPLE = 3 * D
WIN = 256
PADDED = TRIPLE + 128
WIDE = D + 128
ROWS = 256
CHUNK = 32
SLOTS = 8
CHIPS = 4
PAIR = 2 * CHUNK
HALVES = 2
STEP = 16
SPAN = 128
EARLY = 768
TILE = 256
BLOCK = 88
HALF = 768
EPSILON = 1e-06
SCALING = HEAD_DIM ** (-0.5)
MASKED = -1e30

BF = jnp.bfloat16
F32 = jnp.float32


def shape(dims, dtype):
    return jax.ShapeDtypeStruct(dims, dtype)


def call(body, outs, scratch=(), in_specs=None, mib=16, flops=0, data=0, name=None):
    extra = {} if in_specs is None else {"in_specs": in_specs}
    return pl.pallas_call(
        body,
        out_shape=outs,
        scratch_shapes=list(scratch),
        compiler_params=pltpu.CompilerParams(vmem_limit_bytes=mib << 20),
        cost_estimate=pl.CostEstimate(flops=flops, bytes_accessed=data, transcendentals=0),
        name=name,
        **extra,
    )


VMEM = pl.BlockSpec(memory_space=pltpu.VMEM)
SMEM = pl.BlockSpec(memory_space=pltpu.SMEM)
HBM = pl.BlockSpec(memory_space=pl.ANY)


def head_window(head):
    first = (head * HEAD_DIM) // 128 * 128
    offset = head * HEAD_DIM - first
    lane = lax.broadcasted_iota(jnp.int32, (1, WIN), 1)
    return first, (lane >= offset) & (lane < offset + HEAD_DIM)


def keep(lanes, values):
    return jnp.where(lanes, values, jnp.zeros_like(values))


def normalize(rows):
    values = rows.astype(F32)
    centered = values - jnp.mean(values, axis=-1, keepdims=True)
    inv_std = lax.rsqrt(jnp.mean(centered * centered, axis=-1, keepdims=True) + EPSILON)
    return centered * inv_std, inv_std


def place():
    me = lax.axis_index("seq")
    return me // 2, me % 2


def part_rows(chip, core):
    return pl.ds(pl.multiple_of((2 * chip + core) * CHUNK, CHUNK), CHUNK)


def split_body(rows_ref, *refs):
    clip_ref, (mine_ref, theirs_ref) = refs[:-2], refs[-2:]
    chip, core = place()
    for j in range(CHIPS):
        mine_ref[j, :, pl.ds(0, D)] = rows_ref[part_rows(chip ^ j, core), :]
        theirs_ref[j, :, pl.ds(0, D)] = rows_ref[part_rows(chip ^ j, 1 - core), :]
    if clip_ref:
        clip = jnp.full((CHIPS, CHUNK, 128), clip_ref[0][0, 0], jnp.int32).astype(F32).astype(BF)
        mine_ref[:, :, pl.ds(D, 128)] = clip
        theirs_ref[:, :, pl.ds(D, 128)] = clip


def merge_body(mine_ref, other_ref, *refs):
    out_refs = refs[-CHIPS:]
    _, core = place()
    for j in range(CHIPS):
        out_refs[j][pl.ds(pl.multiple_of(core * CHUNK, CHUNK), CHUNK), :] = mine_ref[j]
        out_refs[j][pl.ds(pl.multiple_of((1 - core) * CHUNK, CHUNK), CHUNK), :] = other_ref[j]


def part_body(*refs):
    mine_ref, theirs_ref = refs[CHIPS:]
    _, core = place()
    for j in range(CHIPS):
        mine_ref[j] = refs[j][pl.ds(pl.multiple_of(core * CHUNK, CHUNK), CHUNK), :]
        theirs_ref[j] = refs[j][pl.ds(pl.multiple_of((1 - core) * CHUNK, CHUNK), CHUNK), :]


def join_body(mine_ref, other_ref, out_ref):
    chip, core = place()
    for j in range(CHIPS):
        out_ref[part_rows(chip ^ j, core), :] = mine_ref[j]
        out_ref[part_rows(chip ^ j, 1 - core), :] = other_ref[j]


def load_body(w_hbm, w_ref, sem):
    copy = pltpu.make_async_copy(w_hbm, w_ref, sem)
    copy.start()
    copy.wait()


def in_half(j, f, half):
    return pl.ds(half * SPAN + (2 * j + f) * STEP, STEP)


def norm_body(*refs):
    xs, (gain_ref, _, normed_ref, clip_ref) = refs[:CHIPS], refs[CHIPS:]
    for j in range(CHIPS):
        normalized, _ = normalize(xs[j][:, pl.ds(0, D)])
        normed = (normalized * gain_ref[...]).astype(BF)
        clip = xs[j][:, pl.ds(D, 128)].astype(F32)
        for f in range(2):
            for half in range(HALVES):
                first = f * CHUNK + half * STEP
                normed_ref[in_half(j, f, half), :] = normed[first : first + STEP]
            rows = pl.ds((2 * j + f) * STEP, STEP)
            clip_ref[rows, :] = clip[f * CHUNK : f * CHUNK + STEP]


def turn_body(normed_ref, mine_ref, theirs_ref, wide_ref, other_ref):
    core = lax.axis_index("seq") % 2
    for b in range(16):
        block = normed_ref[:, pl.ds(b * BLOCK // 128 * 128, 256 if b < 15 else 128)]
        offset = b * BLOCK % 128
        turned = jnp.transpose(block.astype(F32))[offset : offset + BLOCK]
        slot = lax.axis_index("dp") ^ b
        by_y = slot // 4 * 4 + b % 4
        by_z = slot % 4 * 4 + b // 4
        slot = jnp.where(core == 0, by_y, by_z)
        wide_ref[pl.ds(pl.multiple_of(slot * BLOCK, 8), BLOCK), :] = turned
        slot = jnp.where(core == 0, by_z, by_y)
        other_ref[pl.ds(pl.multiple_of(slot * BLOCK, 8), BLOCK), :] = turned
    mine_ref[...] = wide_ref[...].astype(BF)
    theirs_ref[...] = other_ref[...].astype(BF)


def project_body(clip_ref, normed_ref, wbuf, qkv_ref, soft_ref, prob_ref, bias_ref):
    first = [(0, EARLY), (D, EARLY)]
    rest = {1: (EARLY, D - EARLY), 4: (D + EARLY, D - EARLY)}
    rest.update({7: (2 * D, 512), 10: (2 * D + 512, 512), 13: (2 * D + 1024, 384)})

    def project(start, count):
        cols = pl.ds(start, count)
        out = jnp.dot(normed_ref[...], wbuf[:, cols], preferred_element_type=F32)
        qkv_ref[:, cols] = out.astype(BF)

    row = lax.broadcasted_iota(jnp.int32, (SPAN, SPAN), 0)
    col = lax.broadcasted_iota(jnp.int32, (SPAN, SPAN), 1)
    clip = clip_ref[...]
    kept = (clip == jnp.transpose(clip)) & (row % STEP == col % STEP)
    bias_ref[...] = jnp.where(kept, 0.0, MASKED).astype(F32)
    qkv_ref[:, pl.ds(TRIPLE, 128)] = jnp.zeros((ROWS, 128), BF)
    qkv_ref[:, pl.ds(2 * D, 128)] = jnp.zeros((ROWS, 128), BF)

    for start, count in first:
        project(start, count)

    def attend(head):
        start, lanes = head_window(head)
        for half in range(HALVES):
            rows = pl.ds(half * SPAN, SPAN)
            query = qkv_ref[rows, pl.ds(start, WIN)]
            key = keep(lanes, qkv_ref[rows, pl.ds(D + start, WIN)])
            scores = lax.dot_general(
                key, query, (((1,), (1,)), ((), ())), preferred_element_type=F32
            )
            scores = scores * SCALING + bias_ref[...]
            powers = jnp.exp(scores - jnp.max(scores, axis=0, keepdims=True))
            softmaxed = powers / jnp.sum(powers, axis=0, keepdims=True)
            soft_ref[head, half] = softmaxed
            prob_ref[head, half] = softmaxed.astype(BF)

    for head in range(HEADS):
        attend(head)
        if head in rest:
            project(*rest[head])


def value_body(prob_ref, *refs):
    chunks = refs[:CHIPS]
    dv_ref, mine_ref, theirs_ref, grad_ref, acc_ref = refs[CHIPS:]
    for j in range(CHIPS):
        for f in range(2):
            for half in range(HALVES):
                rows = pl.ds(f * CHUNK + half * STEP, STEP)
                grad_ref[in_half(j, f, half), pl.ds(0, D)] = chunks[j][rows, :]
    grad_ref[:, pl.ds(D, 128)] = jnp.zeros((ROWS, 128), BF)
    acc_ref[...] = jnp.zeros_like(acc_ref)

    def one(head):
        first, lanes = head_window(head)
        for half in range(HALVES):
            at = pl.ds(half * SPAN, SPAN), pl.ds(first, WIN)
            grad = keep(lanes, grad_ref[at])
            acc_ref[at] += jnp.dot(prob_ref[head, half], grad, preferred_element_type=F32)

    for head in range(HEADS):
        one(head)
    dv_ref[...] = acc_ref[:, pl.ds(0, D)].astype(BF)
    core = lax.axis_index("seq") % 2
    lead = D - HALF
    mine_ref[...] = dv_ref[:, pl.ds(pl.multiple_of(core * lead, 128), HALF)]
    theirs_ref[...] = dv_ref[:, pl.ds(pl.multiple_of((1 - core) * lead, 128), HALF)]


def own_body(nt_ref, dv_ref, out_ref):
    for tile in range(HALF // TILE):
        cols = pl.ds(tile * TILE, TILE)
        out_ref[:, cols] = jnp.dot(nt_ref[...], dv_ref[:, cols], preferred_element_type=F32)


def weight_body(own_ref, nt_other_ref, dv_other_ref, *out_refs):
    for tile in range(HALF // TILE):
        cols = pl.ds(tile * TILE, TILE)
        term = jnp.dot(nt_other_ref[...], dv_other_ref[:, cols], preferred_element_type=F32)
        term += own_ref[:, cols]
        for j in range(4):
            out = out_refs[j]
            out[:, cols] = term[j * 4 * BLOCK : (j + 1) * 4 * BLOCK].astype(out.dtype)


def second_body(*refs):
    parts, gains, out_ref = refs[:4], refs[4:6], refs[6]
    gain = gains[0][...]
    for g in gains[1:]:
        gain = gain + g[...]
    gain = jnp.concatenate([gain, jnp.zeros((1, 2 * HALF - D), F32)], axis=1)
    rest = jnp.concatenate([gain[:, :HALF], gain[:, HALF:]], axis=0)
    total = parts[0][...]
    for part in parts[1:]:
        total = total + part[...].astype(F32)
    for i in range(16):
        rows = jnp.concatenate([total[i * 22 : i * 22 + 22], rest], axis=0)
        out_ref[i] = rows.astype(BF)


def third_body(parts_ref, mine_ref, theirs_ref):
    total = parts_ref[0].astype(F32)
    for i in range(1, 16):
        total = total + parts_ref[i].astype(F32)
    rest = jnp.concatenate([total[22:24], jnp.zeros((3, HALF), F32)], axis=0)
    low = jnp.concatenate([total[:11], rest], axis=0)
    high = jnp.concatenate([total[11:22], rest], axis=0)
    core = lax.axis_index("seq") % 2
    mine_ref[...] = jnp.where(core == 0, low, high)
    theirs_ref[...] = jnp.where(core == 0, high, low)


def last_body(factor):
    def body(mine_ref, other_ref, out_ref, gain_ref):
        core = lax.axis_index("seq") % 2
        mine, other = mine_ref[...] * factor, other_ref[...] * factor
        first = jnp.where(core == 0, mine, other)
        second = jnp.where(core == 0, other, mine)
        gain = (first + second)[11:13]
        out_ref[:, pl.ds(0, HALF)] = first[:11]
        out_ref[:, pl.ds(HALF, D - HALF)] = second[:11, 2 * HALF - D :]
        gain_ref[pl.ds(0, HALF)] = gain[0]
        gain_ref[pl.ds(HALF, D - HALF)] = gain[1, : D - HALF]

    return body


def input_body(*refs):
    xs, refs = refs[:CHIPS], refs[CHIPS:]
    qkv_ref, soft_ref, grad_ref, dv_ref, gain_ref, wbuf = refs[:6]
    outs, gain_out = refs[6 : 6 + CHIPS], refs[6 + CHIPS]
    dq_ref, dk_ref, g_ref, dn_ref = refs[7 + CHIPS :]
    tiles = [(0, 512), (512, 512), (1024, 384)]
    sides = [pl.ds(2 * D, D), pl.ds(0, 2 * D)]

    dq_ref[...] = jnp.zeros_like(dq_ref)
    dk_ref[...] = jnp.zeros_like(dk_ref)
    across = (((1,), (1,)), ((), ()))

    def one(head):
        first, lanes = head_window(head)
        lane = pl.ds(first, WIN)
        query = keep(lanes, qkv_ref[:, lane])
        key = keep(lanes, qkv_ref[:, pl.ds(D + first, WIN)])
        value = keep(lanes, qkv_ref[:, pl.ds(2 * D + first, WIN)])
        parts = []
        for half in range(HALVES):
            d_probs = lax.dot_general(
                value[half * SPAN : (half + 1) * SPAN],
                grad_ref[pl.ds(half * SPAN, SPAN), lane],
                across,
                preferred_element_type=F32,
            )
            softmaxed = soft_ref[head, half]
            row_dot = jnp.sum(softmaxed * d_probs, axis=0, keepdims=True)
            parts.append((softmaxed * (d_probs - row_dot) * SCALING).astype(BF))
        none = jnp.zeros((SPAN, SPAN), BF)
        d_scores = jnp.concatenate(
            [jnp.concatenate([parts[0], none], 1), jnp.concatenate([none, parts[1]], 1)], 0
        )
        dk_ref[:, lane] += jnp.dot(d_scores, query, preferred_element_type=F32)
        dq_ref[:, lane] += lax.dot_general(
            d_scores, key, (((0,), (0,)), ((), ())), preferred_element_type=F32
        )

    for head in range(HEADS):
        one(head)
        if head % 4 == 3 and head < 15:
            rows = pl.ds(*tiles[head // 4])
            dn_ref[:, rows] = lax.dot_general(
                dv_ref[...], wbuf[rows, sides[0]], across, preferred_element_type=F32
            )
    g_ref[:, pl.ds(0, D)] = dq_ref[:, pl.ds(0, D)].astype(BF)
    g_ref[:, pl.ds(D, D)] = dk_ref[:, pl.ds(0, D)].astype(BF)
    for tile in tiles:
        rows = pl.ds(*tile)
        dn_ref[:, rows] += lax.dot_general(
            g_ref[...], wbuf[rows, sides[1]], across, preferred_element_type=F32
        )
    gain = gain_ref[...]
    gain_sum = jnp.zeros((1, D), F32)
    for j, f, half in itertools.product(range(CHIPS), range(2), range(HALVES)):
        rows = pl.ds(f * CHUNK + half * STEP, STEP)
        normalized, inv_std = normalize(xs[j][rows, pl.ds(0, D)])
        d_normed = dn_ref[in_half(j, f, half), :]
        gain_sum = gain_sum + jnp.sum(d_normed * normalized, axis=0, keepdims=True)
        d_hat = d_normed * gain
        first_mean = jnp.mean(d_hat, axis=-1, keepdims=True)
        second_mean = jnp.mean(d_hat * normalized, axis=-1, keepdims=True)
        out = inv_std * (d_hat - first_mean - normalized * second_mean)
        outs[j][rows, :] = out.astype(BF)
    gain_out[...] = gain_sum


def swap_seq(value, k):
    return lax.ppermute(value, "seq", [(i, i ^ k) for i in range(SLOTS)])


def swap_plane(value, j):
    pairs = []
    for dp in range(16):
        for seq in range(SLOTS):
            pairs.append((dp * SLOTS + seq, (dp ^ (4 * j if seq % 2 == 0 else j)) * SLOTS + seq))
    return lax.ppermute(value, ("dp", "seq"), pairs)


def exchange_plane(blocks):
    groups = []
    for core in range(2):
        for i in range(4):
            plane = [4 * i + j if core == 0 else 4 * j + i for j in range(4)]
            groups.append([dp * SLOTS + 2 * x + core for dp in plane for x in range(4)])
    return lax.all_to_all(
        blocks, ("dp", "seq"), split_axis=0, concat_axis=0, tiled=True, axis_index_groups=groups
    )


def swap_chips(chunks):
    moved = {j: swap_seq(chunks[j], 2 * j) for j in (1, 3, 2)}
    return [chunks[0]] + [moved[j] for j in range(1, CHIPS)]


def spread(rows, *clip, after=()):
    width = D + 128 * len(clip)
    mine, theirs = call(
        split_body,
        [shape((CHIPS, CHUNK, width), BF)] * 2,
        in_specs=[VMEM] + [SMEM] * len(clip),
        mib=8,
        data=10**6,
        name="split",
    )(rows, *clip)
    chunks = call(
        merge_body,
        [shape((PAIR, width), BF)] * CHIPS,
        in_specs=[VMEM, VMEM] + [pl.BlockSpec(memory_space=pl.ANY)] * len(after),
        mib=8,
        data=10**6,
        name="merge",
    )(mine, swap_seq(theirs, 1), *after)
    return swap_chips(chunks)


def gather(chunks):
    mine, theirs = call(
        part_body,
        [shape((CHIPS, CHUNK, D), BF)] * 2,
        mib=8,
        flops=2 * 10**10,
        data=10**6,
        name="part",
    )(*swap_chips(chunks))
    return call(join_body, shape((ROWS, D), BF), mib=8, data=10**6, name="join")(
        mine, swap_seq(theirs, 1)
    )


def four(rank, dims):
    return [shape(dims, F32)] + [shape(dims, BF)] * (rank - 1)


def shards(block_input, norm_gain, qkv_weight, frame_clip, out_grad):
    factor = 32768 ** (-0.5)
    gain = norm_gain.reshape(1, D)

    x = spread(block_input.reshape(ROWS, D), frame_clip)
    grads = spread(out_grad.reshape(ROWS, D))

    weight = call(
        load_body,
        shape((D, TRIPLE), BF),
        scratch=[pltpu.SemaphoreType.DMA(())],
        in_specs=[HBM],
        mib=2,
        data=24 * 10**6,
        name="load",
    )(qkv_weight)
    normed, clips = call(
        norm_body,
        [shape((ROWS, D), BF), shape((SPAN, 128), F32)],
        in_specs=[VMEM] * (CHIPS + 1) + [pl.BlockSpec(memory_space=pl.ANY)],
        mib=8,
        data=10**6,
        name="norm",
    )(*x, gain, weight)
    nt, nt_sent = call(
        turn_body,
        [shape((D, ROWS), BF)] * 2,
        scratch=[pltpu.VMEM((D, ROWS), F32)] * 2,
        mib=8,
        data=4 * 10**6,
        name="turn",
    )(normed)
    nt_other = swap_seq(nt_sent, 1)
    qkv, soft, probs = call(
        project_body,
        [
            shape((ROWS, PADDED), BF),
            shape((HEADS, HALVES, SPAN, SPAN), F32),
            shape((HEADS, HALVES, SPAN, SPAN), BF),
        ],
        scratch=[
            pltpu.VMEM((SPAN, SPAN), F32),
        ],
        mib=16,
        flops=5 * 10**9,
        data=40 * 10**6,
        name="project",
    )(clips, normed, weight)

    d_value, mine, theirs, grad_wide = call(
        value_body,
        [
            shape((ROWS, D), BF),
            shape((ROWS, HALF), BF),
            shape((ROWS, HALF), BF),
            shape((ROWS, WIDE), BF),
        ],
        scratch=[pltpu.VMEM((ROWS, WIDE), F32)],
        mib=16,
        flops=10**9,
        data=5 * 10**6,
        name="value",
    )(probs, *grads)
    other = swap_seq(theirs, 1)
    own = call(
        own_body, shape((D, HALF), F32), mib=16, flops=5 * 10**8, data=6 * 10**6, name="own"
    )(nt, mine)
    terms = call(
        weight_body,
        four(4, (4 * BLOCK, HALF)),
        mib=16,
        flops=11 * 10**8,
        data=6 * 10**6,
        name="weight",
    )(own, nt_other, other)
    terms = [terms[0]] + [swap_plane(terms[j], j) for j in range(1, 4)]

    results = call(
        input_body,
        [shape((PAIR, D), BF)] * CHIPS + [shape((1, D), F32)],
        scratch=[
            pltpu.VMEM((ROWS, WIDE), F32),
            pltpu.VMEM((ROWS, WIDE), F32),
            pltpu.VMEM((ROWS, 2 * D), BF),
            pltpu.VMEM((ROWS, D), F32),
        ],
        mib=16,
        flops=6 * 10**9,
        data=20 * 10**6,
        name="input",
    )(*x, qkv, soft, grad_wide, d_value, gain, weight)
    returned, gain_term = results[:CHIPS], results[CHIPS]
    gain_term = gain_term + swap_plane(gain_term, 1)
    gains = [gain_term, swap_plane(gain_term, 3)]

    sums = call(second_body, shape((16, 24, HALF), BF), mib=16, data=5 * 10**6, name="second")(
        *terms, *gains
    )
    sums = exchange_plane(sums)
    mine, theirs = call(third_body, [shape((16, HALF), F32)] * 2, mib=8, data=10**6, name="third")(
        sums
    )
    weight_grad, gain_grad = call(
        last_body(factor),
        [shape((11, D), F32), shape((D,), F32)],
        mib=8,
        data=10**5,
        name="last",
    )(mine, swap_seq(theirs, 1))
    input_grad = gather(returned)
    return input_grad.reshape(block_input.shape), weight_grad, gain_grad


def solution(mesh):
    placed = (P("dp", "seq", None, None), P(), P(), P("dp", "seq"), P("dp", "seq", None, None))
    return jax.shard_map(
        shards,
        mesh=mesh,
        in_specs=placed,
        out_specs=(P("dp", "seq", None, None), P(("dp", "seq"), None), P()),
        check_vma=False,
    )
```
